512 devices in a mesh: tm: 16 (over y, x), space: 8 (over z_hi, core), dp: 4 (over z_lo).
Axes of the slice: x: 4, y: 4, z: 16 (z_hi: 4, z_lo: 4; z = z_hi * 4 + z_lo), core: 2. Of those that a mesh axis runs over, the one named last changes fastest.
Arguments:
- projected: bfloat16 [64, 1024, 3, 40, 128], P(('dp', 'tm'), None, None, 'space'), parts along dimension 0, may hold values from -256 to 256
- q_gain: float32 [40, 128], P('space'), may hold values from 0.1 to 1.9
- k_gain: float32 [40, 128], P('space'), may hold values from 0.1 to 1.9
- head_weight: float32 [40, 128], P('space'), may hold values from -0.078125 to 0.078125
- step_scale: float32 [4, 40, 128], P(None, 'space'), may hold values from 0.5 to 1.5
- timestep: int32 [64], P('dp'), parts along dimension 0, may hold values from 0 to 3
- frame_count: int32 [4096], P('dp'), parts along dimension 0, may hold values from 1 to 16
Outputs:
- logits: float32 [64, 1024], P(('dp', 'tm'), 'space'), parts along dimension 0
The draws below stay inside these ranges and needn't reach their ends.
There are 4 independent parts, one for each index of `dp`. The reference program is written for one: setup_inputs(seed, part) draws one part's arguments, and reference() takes and returns one part's arrays. A program takes and returns all parts, laid end to end along the dimension named above; an argument that names none is the same for every part. Nothing has to cross between parts.
All inputs are finite; a program needn't handle non-finite values.
Results may differ from the reference program's by a relative error of at most 0.01.
Values may be sent and summed in bfloat16 or wider, within the bound.
A program may use at most 64 MiB of HBM per device.

```python
import math
import jax
import jax.numpy as jnp
from jax import lax

HEADS = 40
HEAD = 128
PIXELS = 1024
STEPS = 4
FRAMES = 16


def draw_projected(key, part):
    key = jax.random.fold_in(key, 17)
    keys = jax.random.split(key, 3)
    shape = (FRAMES, PIXELS, 3, HEADS, HEAD)
    ramp = 3.0 ** (jnp.arange(HEADS, dtype=jnp.float32) / max(HEADS - 1, 1))
    ramp = ramp[None, None, None, :, None]
    base = jnp.clip(jax.random.normal(keys[0], shape, jnp.float32), -3.0, 3.0)
    row_scale = jnp.exp(jax.random.uniform(keys[1], (FRAMES, PIXELS, 3, 1, 1), jnp.float32, math.log(0.3), math.log(3.0)))
    column_scale = jnp.exp(jax.random.uniform(keys[2], (1, 1, 3, HEADS, HEAD), jnp.float32, math.log(0.3), math.log(3.0))) * ramp
    field = base * row_scale * column_scale
    return field.astype(jnp.bfloat16)


def place_ends(result, own_key, least, high):
    index_at = [jax.random.randint(jax.random.fold_in(own_key, axis), (), 0, length) for axis, length in enumerate(result.shape)]
    widest = result.shape.index(max(result.shape))
    next_to = index_at[:widest] + [(index_at[widest] + 1) % result.shape[widest]] + index_at[widest + 1:]
    return result.at[tuple(index_at)].set(least).at[tuple(next_to)].set(high)


def block_scale(key, extent, pieces, low, top_value):
    loudness, own = 1.0, jax.random.fold_in(key, 6)
    for axis_at, parts in pieces:
        draws = jnp.exp(jax.random.uniform(jax.random.fold_in(own, axis_at), (parts,), jnp.float32, low / len(pieces), top_value / len(pieces)))
        loudness = loudness * jnp.repeat(draws, extent[axis_at] // parts).reshape([-1 if axis == axis_at else 1 for axis in range(len(extent))])
    return loudness


def bell_draw(own_key, dims, scale, reach, cuts=(), held_as=jnp.bfloat16):
    drawn = scale * jax.random.normal(own_key, dims, jnp.float32)
    if cuts:
        drawn = drawn * block_scale(own_key, dims, cuts, -0.22, 0.18)
    return jnp.clip(drawn, -reach, reach).astype(held_as)


def setup_inputs(seed: int = 0, part: int = 0) -> dict:
    splits = jax.random.split(jax.random.key(seed), 8)
    part_keys = jax.random.split(jax.random.fold_in(splits[7], part), 8)
    return {
        "projected": draw_projected(jax.random.fold_in(jax.random.fold_in(splits[7], part), 71), part),
        "q_gain": jnp.clip(1.0 + 0.18 * jax.random.normal(splits[1], (HEADS, HEAD), jnp.float32), 0.1, 1.9),
        "k_gain": jnp.clip(1.0 + 0.18 * jax.random.normal(splits[2], (HEADS, HEAD), jnp.float32), 0.1, 1.9),
        "head_weight": bell_draw(splits[3], (HEADS, HEAD), (HEADS * HEAD) ** -0.5, 0.078125, ((0, 8),), jnp.float32),
        "step_scale": jnp.clip(0.5 + 1.0 * jax.random.uniform(splits[4], (STEPS, HEADS, HEAD), jnp.float32) ** block_scale(splits[4], (STEPS, HEADS, HEAD), ((1, 8),), -0.2, 0.2), 0.5, 1.5),
        "timestep": place_ends(jax.random.randint(part_keys[5], (FRAMES,), 0, STEPS), jax.random.fold_in(part_keys[5], 1), 0, STEPS - 1).astype(jnp.int32),
        "frame_count": place_ends(jax.random.randint(part_keys[6], (PIXELS,), 1, FRAMES + 1), jax.random.fold_in(part_keys[6], 1), 1, FRAMES).astype(jnp.int32),
    }


epsilon = 1e-06

def reference(projected, q_gain, k_gain, head_weight, step_scale, timestep, frame_count):
    scaling = HEAD ** (-0.5)
    channels = HEADS * HEAD

    def normalize(features_in, gain_row):
        wide_rows = features_in.astype(jnp.float32)
        sum_squares = lax.optimization_barrier(jnp.sum(wide_rows * wide_rows, axis=(1, 2), keepdims=True))
        return (wide_rows * lax.rsqrt(sum_squares / channels + epsilon) * gain_row).astype(jnp.bfloat16)

    def spatial_head(trio):
        query_head, key_head, value_head = trio
        scores = jnp.dot(query_head, key_head.T, preferred_element_type=jnp.float32) * scaling
        row_max = lax.optimization_barrier(jnp.max(scores, axis=1, keepdims=True))
        exponent = jnp.exp(scores - row_max)
        weights = (exponent / lax.optimization_barrier(jnp.sum(exponent, axis=1, keepdims=True))).astype(jnp.bfloat16)
        return jnp.dot(weights, value_head, preferred_element_type=jnp.float32).astype(jnp.bfloat16)

    def frame_pass(frame_rows):
        q_heads = jnp.swapaxes(normalize(frame_rows[:, 0], q_gain), 0, 1)
        k_heads = jnp.swapaxes(normalize(frame_rows[:, 1], k_gain), 0, 1)
        v_heads = jnp.swapaxes(frame_rows[:, 2], 0, 1)
        spatial = lax.map(spatial_head, (q_heads, k_heads, v_heads))
        return (q_heads, k_heads, spatial)
    q_all, k_all, spatial_all = lax.map(frame_pass, projected)
    spatial_all = lax.optimization_barrier(spatial_all)
    live_frames = jnp.arange(FRAMES, dtype=jnp.int32)[None, :] < frame_count.astype(jnp.int32)[:, None]

    def temporal_head(trio):
        query_head, key_head, value_head = trio
        scores = jnp.einsum('fpe,gpe->pfg', query_head.astype(jnp.float32), key_head.astype(jnp.float32)) * scaling
        scores = jnp.where(live_frames[:, None, :], scores, -1e+30)
        row_max = lax.optimization_barrier(jnp.max(scores, axis=2, keepdims=True))
        exponent = jnp.exp(scores - row_max)
        weights = (exponent / lax.optimization_barrier(jnp.sum(exponent, axis=2, keepdims=True))).astype(jnp.bfloat16)
        return jnp.einsum('pfg,gpe->fpe', weights.astype(jnp.float32), value_head.astype(jnp.float32)).astype(jnp.bfloat16)
    temporal_all = lax.map(temporal_head, (jnp.swapaxes(q_all, 0, 1), jnp.swapaxes(k_all, 0, 1), jnp.swapaxes(spatial_all, 0, 1)))
    temporal_all = lax.optimization_barrier(temporal_all)
    frame_scales = jnp.take(step_scale, timestep.astype(jnp.int32), axis=0)
    frame_scales = jnp.swapaxes(frame_scales, 0, 1)
    combined = jnp.swapaxes(spatial_all, 0, 1).astype(jnp.float32) + temporal_all.astype(jnp.float32)
    modulated = combined * frame_scales[:, :, None, :]
    dot_total = lax.optimization_barrier(jnp.sum(modulated * head_weight[:, None, None, :], axis=(0, 3)))
    square_total = lax.optimization_barrier(jnp.sum(modulated * modulated, axis=(0, 3)))
    return dot_total * lax.rsqrt(square_total / channels + epsilon)
```

```python
import functools
import math

import jax
import jax.numpy as jnp
from jax import lax
from jax.experimental import pallas as pl
from jax.experimental.pallas import tpu as pltpu
from jax.sharding import PartitionSpec as P

HEADS = 40
HEAD = 128
PIXELS = 1024
FRAMES = 16
STEPS = 4
SPACE = 8
OWN_HEADS = HEADS // SPACE
BLOCK = PIXELS // FRAMES
ROWS = PIXELS // 128
QUERY_TILE = 256
GROUP = 8
GROUPS = BLOCK // GROUP
SIDE = 4

EPSILON = 1e-06
CHANNELS = HEADS * HEAD
SCALE_LOG2E = HEAD ** (-0.5) * math.log2(math.e)
MESH = pl.DeviceIdType.MESH


def offsets():
    def hops(o):
        return min(o[0], SIDE - o[0]) + min(o[1], SIDE - o[1])

    every = [(dy, dx) for dy in range(SIDE) for dx in range(SIDE) if (dy, dx) != (0, 0)]
    return sorted(every, key=lambda o: -hops(o))


def wait_bytes(ref, sem):
    pltpu.make_async_copy(ref, ref, sem).wait()


def column(row):
    return jnp.transpose(jnp.broadcast_to(row, (128, 128)))


def kernel(
    proj, q_gain, k_gain, head_weight, step_scale, timestep, frame_count,
    out,
    x, qk_in, o_out, o_in, ssq_out, ssq_in, fac_out, fac_in, normed, fcol, mix, scale, z, zpad,
    fin_out, fin_in, gains, weight, steps, live, steps_at, counts,
    local_sem, own_sem, qk_send, qk_recv, ssq_send, ssq_recv, fac_send, fac_recv,
    o_send, o_recv, fin_send, fin_recv, last_send,
):
    me = lax.axis_index("tm")
    sp = lax.axis_index("space")
    dp = lax.axis_index("dp")
    y, xx = me // SIDE, me % SIDE
    peers = [((y + dy) % SIDE) * SIDE + (xx + dx) % SIDE for dy, dx in offsets()]
    half = me % 2

    barrier = pltpu.get_barrier_semaphore()
    for t in peers:
        pl.semaphore_signal(barrier, inc=1, device_id=(t, sp, dp), device_id_type=MESH)
    for d in range(1, SPACE):
        pl.semaphore_signal(barrier, inc=1, device_id=(me, (sp + d) % SPACE, dp), device_id_type=MESH)

    loads = [
        pltpu.make_async_copy(proj.at[0], x.at[0], local_sem.at[0]),
        pltpu.make_async_copy(proj.at[1], x.at[1], local_sem.at[1]),
        pltpu.make_async_copy(proj.at[2], x.at[2], local_sem.at[2]),
        pltpu.make_async_copy(q_gain, gains.at[0], local_sem.at[3]),
        pltpu.make_async_copy(k_gain, gains.at[1], local_sem.at[4]),
        pltpu.make_async_copy(head_weight, weight, local_sem.at[5]),
        pltpu.make_async_copy(step_scale, steps, local_sem.at[6]),
        pltpu.make_async_copy(timestep, steps_at, local_sem.at[7]),
        pltpu.make_async_copy(frame_count, counts, local_sem.at[8]),
    ]
    for load in loads:
        load.start()

    pl.semaphore_wait(barrier, len(peers) + SPACE - 1)

    def rows_of(t):
        return pl.ds(pl.multiple_of(t * BLOCK, BLOCK), BLOCK)

    for t in peers:
        pltpu.make_async_remote_copy(
            proj.at[pl.ds(0, 2), :, rows_of(t)], qk_in.at[me], qk_send, qk_recv,
            device_id=(t, sp, dp), device_id_type=MESH,
        ).start()
    own = pltpu.make_async_copy(proj.at[pl.ds(0, 2), :, rows_of(me)], qk_in.at[me], own_sem)
    own.start()

    for c in range(2):
        loads[c].wait()
        for r in range(ROWS):
            total = jnp.zeros((128, 128), jnp.float32)
            for h in range(OWN_HEADS):
                part = x[c, h, 128 * r : 128 * (r + 1), :].astype(jnp.float32)
                total += part * part
            ssq_out[r, c : c + 1, :] = jnp.sum(jnp.transpose(total), axis=0, keepdims=True)
    for d in range(1, SPACE):
        pltpu.make_async_remote_copy(
            ssq_out, ssq_in.at[sp], ssq_send, ssq_recv,
            device_id=(me, (sp + d) % SPACE, dp), device_id_type=MESH,
        ).start()
    ssq_in[sp] = ssq_out[...]

    for load in loads[3:]:
        load.wait()
    lane = lax.broadcasted_iota(jnp.int32, (1, 128), 1)
    for b in range(GROUPS):
        row = jnp.zeros((1, 128), jnp.int32)
        for i in range(GROUP):
            row = jnp.where(lane % GROUP == i, counts[me * BLOCK + b * GROUP + i], row)
        live[b : b + 1, :] = row
    for f in range(FRAMES):
        scale[:, f : f + 1, :] = steps[:, pl.ds(steps_at[f], 1), :]
    z[...] = jnp.zeros_like(z)
    zpad[...] = jnp.zeros_like(zpad)

    wait_bytes(ssq_in.at[pl.ds(0, SPACE - 1)], ssq_recv)
    sums = ssq_in[0]
    for s in range(1, SPACE):
        sums += ssq_in[s]
    fac_out[...] = lax.rsqrt(sums / CHANNELS + EPSILON)
    for t in peers:
        pltpu.make_async_remote_copy(
            fac_out.at[t // 2], fac_in.at[me], fac_send, fac_recv,
            device_id=(t, sp, dp), device_id_type=MESH,
        ).start()
    fac_in[me] = fac_out[me // 2]

    for c in range(2):
        for r in range(ROWS):
            factor = column(fac_out[r, c : c + 1, :])
            for h in range(OWN_HEADS):
                rows = slice(128 * r, 128 * (r + 1))
                part = x[c, h, rows, :].astype(jnp.float32) * factor
                normed[c, h, rows, :] = (part * gains[c, h : h + 1, :]).astype(jnp.bfloat16)

    loads[2].wait()

    def spatial_head(h, carry):
        def tile(i, carry):
            rows = pl.ds(pl.multiple_of(i * QUERY_TILE, QUERY_TILE), QUERY_TILE)
            scores = lax.dot_general(
                normed[0, h, rows, :], normed[1, h], (((1,), (1,)), ((), ())),
                preferred_element_type=jnp.float32,
            )
            top = jnp.max(scores, axis=1, keepdims=True)
            exponent = jnp.exp2((scores - top) * SCALE_LOG2E)
            share = 1.0 / jnp.sum(exponent, axis=1, keepdims=True)
            weights = (exponent * share).astype(jnp.bfloat16)
            o_out[h, rows, :] = jnp.dot(
                weights, x[2, h], preferred_element_type=jnp.float32
            ).astype(jnp.bfloat16)
            return carry

        lax.fori_loop(0, PIXELS // QUERY_TILE, tile, 0)
        for t in peers:
            pltpu.make_async_remote_copy(
                o_out.at[h, rows_of(t)], o_in.at[h, me], o_send.at[h], o_recv.at[h],
                device_id=(t, sp, dp), device_id_type=MESH,
            ).start()
        o_in[h, me] = o_out[h, rows_of(me), :]
        return carry

    lax.fori_loop(0, OWN_HEADS, spatial_head, 0)

    wait_bytes(fac_in.at[pl.ds(0, FRAMES - 1)], fac_recv)
    for c in range(2):
        for f in range(FRAMES):
            fcol[c, f] = column(fac_in[f, c : c + 1, :])
    own.wait()
    wait_bytes(qk_in.at[pl.ds(0, FRAMES - 1)], qk_recv)
    side = FRAMES * GROUP
    at_row = lax.broadcasted_iota(jnp.int32, (side, side), 0)
    at_lane = lax.broadcasted_iota(jnp.int32, (side, side), 1)
    same = (at_row % GROUP) == (at_lane % GROUP)
    key_frame = at_lane // GROUP
    my_half = pl.ds(pl.multiple_of(half * BLOCK, BLOCK), BLOCK)

    def temporal_weights(h, carry):
        wide = []
        for c in range(2):
            part = qk_in[:, c, h].astype(jnp.float32) * fcol[c, :, my_half, :]
            wide.append(part * gains[c, pl.ds(h, 1), :].reshape(1, 1, HEAD))
        for b in range(GROUPS):
            queries, keys = (
                w[:, GROUP * b : GROUP * (b + 1), :].reshape(side, HEAD).astype(jnp.bfloat16)
                for w in wide
            )
            scores = lax.dot_general(
                queries, keys, (((1,), (1,)), ((), ())), preferred_element_type=jnp.float32
            )
            seen = same & (key_frame < live[b : b + 1, :])
            scores = jnp.where(seen, scores, -1e30)
            top = jnp.max(scores, axis=1, keepdims=True)
            exponent = jnp.exp2((scores - top) * SCALE_LOG2E)
            share = 1.0 / jnp.sum(exponent, axis=1, keepdims=True)
            mix[h, b] = (exponent * share).astype(jnp.bfloat16)
        return carry

    lax.fori_loop(0, OWN_HEADS, temporal_weights, 0)

    at_frame = lax.broadcasted_iota(jnp.int32, (FRAMES, GROUP, 128), 0)
    at_lane3 = lax.broadcasted_iota(jnp.int32, (FRAMES, GROUP, 128), 2)
    dot_lane = at_frame == at_lane3
    square_lane = at_frame + FRAMES == at_lane3

    def temporal_head(h, carry):
        wait_bytes(o_in.at[h, pl.ds(0, FRAMES - 1)], o_recv.at[h])
        spatial = o_in[h].astype(jnp.float32)
        row_scale = scale[h].reshape(FRAMES, 1, HEAD)
        row_weight = weight[pl.ds(h, 1), :].reshape(1, 1, HEAD)
        for b in range(GROUPS):
            pixels = slice(GROUP * b, GROUP * (b + 1))
            block = spatial[:, pixels, :]
            mixed = jnp.dot(
                mix[h, b], block.reshape(side, HEAD).astype(jnp.bfloat16),
                preferred_element_type=jnp.float32,
            ).astype(jnp.bfloat16).astype(jnp.float32)
            modulated = (block + mixed.reshape(FRAMES, GROUP, HEAD)) * row_scale
            dots = jnp.sum(modulated * row_weight, axis=2, keepdims=True)
            squares = jnp.sum(modulated * modulated, axis=2, keepdims=True)
            placed = jnp.where(dot_lane, dots, 0.0) + jnp.where(square_lane, squares, 0.0)
            z[pixels, :] += jnp.sum(placed, axis=0)
        return carry

    lax.fori_loop(0, OWN_HEADS, temporal_head, 0)

    zpad[my_half, :] = z[...]
    turned = jnp.transpose(zpad[...])
    for f in range(FRAMES):
        fin_out[f, 0:1, :] = turned[f : f + 1, :]
        fin_out[f, 1:2, :] = turned[FRAMES + f : FRAMES + f + 1, :]
    owner = me // 2
    slot = half * SPACE + sp
    for t in peers:
        pltpu.make_async_remote_copy(
            fin_out.at[t], fin_in.at[slot], fin_send, fin_recv,
            device_id=(t, owner, dp), device_id_type=MESH,
        ).start()

    @pl.when(sp == owner)
    def _():
        here = pltpu.make_async_copy(fin_out.at[me], fin_in.at[slot], fin_recv)
        here.start()

    @pl.when(sp != owner)
    def _():
        away = pltpu.make_async_remote_copy(
            fin_out.at[me], fin_in.at[slot], last_send, fin_recv,
            device_id=(me, owner, dp), device_id_type=MESH,
        )
        away.start()
        away.wait_send()

    wait_bytes(qk_in.at[pl.ds(0, FRAMES - 1)], qk_send)
    wait_bytes(ssq_in.at[pl.ds(0, SPACE - 1)], ssq_send)
    wait_bytes(fac_in.at[pl.ds(0, FRAMES - 1)], fac_send)
    for h in range(OWN_HEADS):
        wait_bytes(o_in.at[h, pl.ds(0, FRAMES - 1)], o_send.at[h])
    wait_bytes(fin_out.at[pl.ds(0, FRAMES - 1)], fin_send)
    wait_bytes(fin_in, fin_recv)
    totals = jnp.sum(fin_in[...], axis=0)
    out[...] = totals[0:1, :] * lax.rsqrt(totals[1:2, :] / CHANNELS + EPSILON)


def on_device(projected, q_gain, k_gain, head_weight, step_scale, timestep, frame_count):
    proj = jnp.transpose(projected[0], (1, 2, 0, 3))
    steps = jnp.transpose(step_scale, (1, 0, 2))
    any_space = pl.BlockSpec(memory_space=pl.ANY)
    bf16, f32 = jnp.bfloat16, jnp.float32
    dma = pltpu.SemaphoreType.DMA
    return pl.pallas_call(
        kernel,
        out_shape=jax.ShapeDtypeStruct((1, 128), f32),
        in_specs=[any_space] * 7,
        out_specs=pl.BlockSpec(memory_space=pltpu.VMEM),
        scratch_shapes=[
            pltpu.VMEM((3, OWN_HEADS, PIXELS, HEAD), bf16),
            pltpu.VMEM((FRAMES, 2, OWN_HEADS, BLOCK, HEAD), bf16),
            pltpu.VMEM((OWN_HEADS, PIXELS, HEAD), bf16),
            pltpu.VMEM((OWN_HEADS, FRAMES, BLOCK, HEAD), bf16),
            pltpu.VMEM((ROWS, 2, 128), f32),
            pltpu.VMEM((SPACE, ROWS, 2, 128), f32),
            pltpu.VMEM((ROWS, 2, 128), f32),
            pltpu.VMEM((FRAMES, 2, 128), f32),
            pltpu.VMEM((2, OWN_HEADS, PIXELS, HEAD), bf16),
            pltpu.VMEM((2, FRAMES, 128, 128), f32),
            pltpu.VMEM((OWN_HEADS, GROUPS, 128, 128), bf16),
            pltpu.VMEM((OWN_HEADS, FRAMES, HEAD), f32),
            pltpu.VMEM((BLOCK, 128), f32),
            pltpu.VMEM((128, 128), f32),
            pltpu.VMEM((FRAMES, 2, 128), f32),
            pltpu.VMEM((FRAMES, 2, 128), f32),
            pltpu.VMEM((2, OWN_HEADS, HEAD), f32),
            pltpu.VMEM((OWN_HEADS, HEAD), f32),
            pltpu.VMEM((OWN_HEADS, STEPS, HEAD), f32),
            pltpu.VMEM((GROUPS, 128), jnp.int32),
            pltpu.SMEM((FRAMES,), jnp.int32),
            pltpu.SMEM((PIXELS,), jnp.int32),
            dma((9,)), dma, dma, dma, dma, dma, dma, dma,
            dma((OWN_HEADS,)), dma((OWN_HEADS,)), dma, dma, dma,
        ],
        compiler_params=pltpu.CompilerParams(
            collective_id=0, has_side_effects=True, vmem_limit_bytes=56 * 2**20
        ),
        cost_estimate=pl.CostEstimate(
            flops=3_000_000_000, bytes_accessed=8_000_000, transcendentals=6_000_000
        ),
        name="space_time_attention",
    )(proj, q_gain, k_gain, head_weight, steps, timestep, frame_count)


def solution(mesh):
    in_specs = (
        P(("dp", "tm"), None, None, "space", None),
        P("space", None),
        P("space", None),
        P("space", None),
        P(None, "space", None),
        P("dp"),
        P("dp"),
    )
    out_specs = P(("dp", "tm"), "space")
    return jax.shard_map(
        on_device, mesh=mesh, in_specs=in_specs, out_specs=out_specs, check_vma=False
    )
```

```python
import functools
import math

import jax
import jax.numpy as jnp
from jax import lax
from jax.experimental import pallas as pl
from jax.experimental.pallas import tpu as pltpu
from jax.sharding import PartitionSpec as P

HEADS = 40
HEAD = 128
PIXELS = 1024
FRAMES = 16
STEPS = 4
SPACE = 8
OWN_HEADS = HEADS // SPACE
BLOCK = PIXELS // FRAMES
ROWS = PIXELS // 128
QUERY_TILE = 256
GROUP = 8
GROUPS = BLOCK // GROUP
EARLY_HEADS = 3
SIDE = 4

EPSILON = 1e-06
CHANNELS = HEADS * HEAD
SCALE_LOG2E = HEAD ** (-0.5) * math.log2(math.e)
MESH = pl.DeviceIdType.MESH


OFFSETS = (
    (2, 2), (2, 3), (2, 1), (3, 2), (1, 2), (2, 0), (0, 2), (3, 1),
    (1, 3), (3, 3), (1, 1), (3, 0), (1, 0), (0, 3), (0, 1),
)


def fold(i):
    return i + i // 2 - 2 * (i // 3)


def space_at(rank):
    return 2 * fold(rank // 2) + rank % 2


def wait_bytes(ref, sem):
    pltpu.make_async_copy(ref, ref, sem).wait()


def column(row):
    return jnp.transpose(jnp.broadcast_to(row, (128, 128)))


def kernel(
    proj, q_gain, k_gain, head_weight, step_scale, timestep, frame_count,
    out,
    x, qk_in, own_qk, o_out, o_in, ssq_out, ssq_in, fac_out, fac_in, normed, fcol, mix, scale, z,
    fin_out, fin_in, gains, weight, steps, live, steps_at, counts,
    local_sem, own_sem, qk_send, qk_recv, ssq_send, ssq_recv, fac_send, fac_recv,
    o_send, o_recv, fin_send, fin_recv, last_send, entered,
):
    me = lax.axis_index("tm")
    sp = lax.axis_index("space")
    dp = lax.axis_index("dp")
    y, xx = me // SIDE, me % SIDE
    down = [SIDE * jnp.where(y + d >= SIDE, y + d - SIDE, y + d) for d in range(SIDE)]
    along = [jnp.where(xx + d >= SIDE, xx + d - SIDE, xx + d) for d in range(SIDE)]
    peers = [down[dy] + along[dx] for dy, dx in OFFSETS]
    half = me % 2

    loads = [
        pltpu.make_async_copy(proj.at[0], x.at[0], local_sem.at[0]),
        pltpu.make_async_copy(proj.at[1], x.at[1], local_sem.at[1]),
        pltpu.make_async_copy(proj.at[2], x.at[2], local_sem.at[2]),
        pltpu.make_async_copy(q_gain, gains.at[0], local_sem.at[3]),
        pltpu.make_async_copy(k_gain, gains.at[1], local_sem.at[4]),
        pltpu.make_async_copy(head_weight, weight, local_sem.at[5]),
        pltpu.make_async_copy(step_scale, steps, local_sem.at[6]),
        pltpu.make_async_copy(timestep, steps_at, local_sem.at[7]),
        pltpu.make_async_copy(frame_count, counts, local_sem.at[8]),
    ]
    for load in loads[:2]:
        load.start()

    barrier = pltpu.get_barrier_semaphore()
    for t in peers:
        pl.semaphore_signal(barrier, inc=1, device_id=(t, sp, dp), device_id_type=MESH)
    rank = 2 * fold(sp // 2) + sp % 2

    def announce(r, carry):
        pl.semaphore_signal(
            barrier, inc=1, device_id=(me, space_at(r), dp), device_id_type=MESH
        )
        return carry

    lax.fori_loop(rank + 1, SPACE, announce, 0)

    pl.semaphore_wait(barrier, len(peers) + rank)

    def enter(r, carry):
        pl.semaphore_signal(
            entered, inc=1, device_id=(me, space_at(r), dp), device_id_type=MESH
        )
        return carry

    def send_ssq(r, carry):
        pltpu.make_async_remote_copy(
            ssq_out, ssq_in.at[sp], ssq_send, ssq_recv,
            device_id=(me, space_at(r), dp), device_id_type=MESH,
        ).start()
        return carry

    def rows_of(t):
        return pl.ds(pl.multiple_of(t * BLOCK, BLOCK), BLOCK)

    def send_qk(h):
        for t in peers:
            pltpu.make_async_remote_copy(
                proj.at[pl.ds(0, 2), h, rows_of(t)], qk_in.at[h, me], qk_send.at[h], qk_recv.at[h],
                device_id=(t, sp, dp), device_id_type=MESH,
            ).start()

    send_qk(0)
    lax.fori_loop(0, rank, enter, 0)
    for load in loads[2:]:
        load.start()

    for c in range(2):
        loads[c].wait()
        for r in range(ROWS):
            total = jnp.zeros((128, 128), jnp.float32)
            for h in range(OWN_HEADS):
                part = x[c, h, 128 * r : 128 * (r + 1), :].astype(jnp.float32)
                total += part * part
            ssq_out[r, c : c + 1, :] = jnp.sum(jnp.transpose(total), axis=0, keepdims=True)
    ssq_in[sp] = ssq_out[...]
    lax.fori_loop(0, rank, send_ssq, 0)

    @pl.when(rank < SPACE // 2)
    def _():
        for h in range(1, EARLY_HEADS):
            send_qk(h)

    @pl.when(rank < SPACE - 1)
    def _():
        pl.semaphore_wait(entered, SPACE - 1 - rank)
        lax.fori_loop(rank + 1, SPACE, send_ssq, 0)

    @pl.when(rank >= SPACE // 2)
    def _():
        for h in range(1, EARLY_HEADS):
            send_qk(h)

    for h in range(EARLY_HEADS, OWN_HEADS - 1):
        send_qk(h)
    own = pltpu.make_async_copy(proj.at[pl.ds(0, 2), :, rows_of(me)], own_qk, own_sem)
    own.start()

    for load in loads[3:]:
        load.wait()
    lane = lax.broadcasted_iota(jnp.int32, (1, 128), 1)
    for b in range(GROUPS):
        row = jnp.zeros((1, 128), jnp.int32)
        for i in range(GROUP):
            row = jnp.where(lane % GROUP == i, counts[me * BLOCK + b * GROUP + i], row)
        live[b : b + 1, :] = row
    for f in range(FRAMES):
        scale[:, f : f + 1, :] = steps[:, pl.ds(steps_at[f], 1), :]
    z[...] = jnp.zeros_like(z)

    wait_bytes(ssq_in.at[pl.ds(0, SPACE - 1)], ssq_recv)
    sums = ssq_in[0]
    for s in range(1, SPACE):
        sums += ssq_in[s]
    fac_out[...] = lax.rsqrt(sums / CHANNELS + EPSILON)
    for t in peers:
        pltpu.make_async_remote_copy(
            fac_out.at[t // 2], fac_in.at[me], fac_send, fac_recv,
            device_id=(t, sp, dp), device_id_type=MESH,
        ).start()
    send_qk(OWN_HEADS - 1)
    fac_in[me] = fac_out[me // 2]

    for c in range(2):
        for r in range(ROWS):
            factor = column(fac_out[r, c : c + 1, :])
            for h in range(OWN_HEADS):
                rows = slice(128 * r, 128 * (r + 1))
                part = x[c, h, rows, :].astype(jnp.float32) * factor
                normed[c, h, rows, :] = (part * gains[c, h : h + 1, :]).astype(jnp.bfloat16)

    loads[2].wait()

    def spatial_head(h, carry):
        def tile(i, carry):
            rows = pl.ds(pl.multiple_of(i * QUERY_TILE, QUERY_TILE), QUERY_TILE)
            scores = lax.dot_general(
                normed[0, h, rows, :], normed[1, h], (((1,), (1,)), ((), ())),
                preferred_element_type=jnp.float32,
            )
            top = jnp.max(scores, axis=1, keepdims=True)
            exponent = jnp.exp2((scores - top) * SCALE_LOG2E)
            share = 1.0 / jnp.sum(exponent, axis=1, keepdims=True)
            weights = (exponent * share).astype(jnp.bfloat16)
            o_out[h, rows, :] = jnp.dot(
                weights, x[2, h], preferred_element_type=jnp.float32
            ).astype(jnp.bfloat16)
            return carry

        lax.fori_loop(0, PIXELS // QUERY_TILE, tile, 0)
        for t in peers:
            pltpu.make_async_remote_copy(
                o_out.at[h, rows_of(t)], o_in.at[h, me], o_send.at[h], o_recv.at[h],
                device_id=(t, sp, dp), device_id_type=MESH,
            ).start()
        o_in[h, me] = o_out[h, rows_of(me), :]
        return carry

    lax.fori_loop(0, OWN_HEADS, spatial_head, 0)

    wait_bytes(fac_in.at[pl.ds(0, FRAMES - 1)], fac_recv)
    for c in range(2):
        for f in range(FRAMES):
            fcol[c, f] = column(fac_in[f, c : c + 1, :])
    own.wait()
    for c in range(2):
        for h in range(OWN_HEADS):
            qk_in[h, me, c] = own_qk[c, h]
    side = FRAMES * GROUP
    at_row = lax.broadcasted_iota(jnp.int32, (side, side), 0)
    at_lane = lax.broadcasted_iota(jnp.int32, (side, side), 1)
    same = (at_row % GROUP) == (at_lane % GROUP)
    key_frame = at_lane // GROUP
    my_half = pl.ds(pl.multiple_of(half * BLOCK, BLOCK), BLOCK)

    def temporal_weights(h, carry):
        wait_bytes(qk_in.at[h, pl.ds(0, FRAMES - 1)], qk_recv.at[h])
        wide = []
        for c in range(2):
            part = qk_in[h, :, c].astype(jnp.float32) * fcol[c, :, my_half, :]
            wide.append(part * gains[c, pl.ds(h, 1), :].reshape(1, 1, HEAD))
        for b in range(GROUPS):
            queries, keys = (
                w[:, GROUP * b : GROUP * (b + 1), :].reshape(side, HEAD).astype(jnp.bfloat16)
                for w in wide
            )
            scores = lax.dot_general(
                queries, keys, (((1,), (1,)), ((), ())), preferred_element_type=jnp.float32
            )
            seen = same & (key_frame < live[b : b + 1, :])
            scores = jnp.where(seen, scores, -1e30)
            top = jnp.max(scores, axis=1, keepdims=True)
            exponent = jnp.exp2((scores - top) * SCALE_LOG2E)
            share = 1.0 / jnp.sum(exponent, axis=1, keepdims=True)
            mix[h, b] = (exponent * share).astype(jnp.bfloat16)
        return carry

    lax.fori_loop(0, OWN_HEADS, temporal_weights, 0)

    at_frame = lax.broadcasted_iota(jnp.int32, (FRAMES, GROUP, 128), 0)
    at_lane3 = lax.broadcasted_iota(jnp.int32, (FRAMES, GROUP, 128), 2)
    dot_lane = at_frame == at_lane3
    square_lane = at_frame + FRAMES == at_lane3

    def temporal_head(h, carry):
        wait_bytes(o_in.at[h, pl.ds(0, FRAMES - 1)], o_recv.at[h])
        spatial = o_in[h].astype(jnp.float32)
        row_scale = scale[h].reshape(FRAMES, 1, HEAD)
        row_weight = weight[pl.ds(h, 1), :].reshape(1, 1, HEAD)
        for b in range(GROUPS):
            pixels = slice(GROUP * b, GROUP * (b + 1))
            block = spatial[:, pixels, :]
            mixed = jnp.dot(
                mix[h, b], block.reshape(side, HEAD).astype(jnp.bfloat16),
                preferred_element_type=jnp.float32,
            ).astype(jnp.bfloat16).astype(jnp.float32)
            modulated = (block + mixed.reshape(FRAMES, GROUP, HEAD)) * row_scale
            dots = jnp.sum(modulated * row_weight, axis=2, keepdims=True)
            squares = jnp.sum(modulated * modulated, axis=2, keepdims=True)
            placed = jnp.where(dot_lane, dots, 0.0) + jnp.where(square_lane, squares, 0.0)
            at = pl.ds(pl.multiple_of(half * BLOCK + GROUP * b, GROUP), GROUP)
            z[at, :] += jnp.sum(placed, axis=0)
        return carry

    lax.fori_loop(0, OWN_HEADS, temporal_head, 0)

    turned = jnp.transpose(z[...])
    for f in range(FRAMES):
        fin_out[f, 0:1, :] = turned[f : f + 1, :]
        fin_out[f, 1:2, :] = turned[FRAMES + f : FRAMES + f + 1, :]
    owner = me // 2
    slot = half * SPACE + sp
    for t in peers:
        pltpu.make_async_remote_copy(
            fin_out.at[t], fin_in.at[slot], fin_send, fin_recv,
            device_id=(t, owner, dp), device_id_type=MESH,
        ).start()

    @pl.when(sp == owner)
    def _():
        here = pltpu.make_async_copy(fin_out.at[me], fin_in.at[slot], fin_recv)
        here.start()

    @pl.when(sp != owner)
    def _():
        away = pltpu.make_async_remote_copy(
            fin_out.at[me], fin_in.at[slot], last_send, fin_recv,
            device_id=(me, owner, dp), device_id_type=MESH,
        )
        away.start()
        away.wait_send()

    wait_bytes(ssq_in.at[pl.ds(0, SPACE - 1)], ssq_send)
    wait_bytes(fac_in.at[pl.ds(0, FRAMES - 1)], fac_send)
    for h in range(OWN_HEADS):
        wait_bytes(qk_in.at[h, pl.ds(0, FRAMES - 1)], qk_send.at[h])
        wait_bytes(o_in.at[h, pl.ds(0, FRAMES - 1)], o_send.at[h])
    wait_bytes(fin_out.at[pl.ds(0, FRAMES - 1)], fin_send)
    wait_bytes(fin_in, fin_recv)
    totals = jnp.sum(fin_in[...], axis=0)
    out[...] = totals[0:1, :] * lax.rsqrt(totals[1:2, :] / CHANNELS + EPSILON)


def on_device(projected, q_gain, k_gain, head_weight, step_scale, timestep, frame_count):
    proj = jnp.transpose(projected[0], (1, 2, 0, 3))
    steps = jnp.transpose(step_scale, (1, 0, 2))
    any_space = pl.BlockSpec(memory_space=pl.ANY)
    bf16, f32 = jnp.bfloat16, jnp.float32
    dma = pltpu.SemaphoreType.DMA
    return pl.pallas_call(
        kernel,
        out_shape=jax.ShapeDtypeStruct((1, 128), f32),
        in_specs=[any_space] * 7,
        out_specs=pl.BlockSpec(memory_space=pltpu.VMEM),
        scratch_shapes=[
            pltpu.VMEM((3, OWN_HEADS, PIXELS, HEAD), bf16),
            pltpu.VMEM((OWN_HEADS, FRAMES, 2, BLOCK, HEAD), bf16),
            pltpu.VMEM((2, OWN_HEADS, BLOCK, HEAD), bf16),
            pltpu.VMEM((OWN_HEADS, PIXELS, HEAD), bf16),
            pltpu.VMEM((OWN_HEADS, FRAMES, BLOCK, HEAD), bf16),
            pltpu.VMEM((ROWS, 2, 128), f32),
            pltpu.VMEM((SPACE, ROWS, 2, 128), f32),
            pltpu.VMEM((ROWS, 2, 128), f32),
            pltpu.VMEM((FRAMES, 2, 128), f32),
            pltpu.VMEM((2, OWN_HEADS, PIXELS, HEAD), bf16),
            pltpu.VMEM((2, FRAMES, 128, 128), f32),
            pltpu.VMEM((OWN_HEADS, GROUPS, 128, 128), bf16),
            pltpu.VMEM((OWN_HEADS, FRAMES, HEAD), f32),
            pltpu.VMEM((128, 128), f32),
            pltpu.VMEM((FRAMES, 2, 128), f32),
            pltpu.VMEM((FRAMES, 2, 128), f32),
            pltpu.VMEM((2, OWN_HEADS, HEAD), f32),
            pltpu.VMEM((OWN_HEADS, HEAD), f32),
            pltpu.VMEM((OWN_HEADS, STEPS, HEAD), f32),
            pltpu.VMEM((GROUPS, 128), jnp.int32),
            pltpu.SMEM((FRAMES,), jnp.int32),
            pltpu.SMEM((PIXELS,), jnp.int32),
            dma((9,)), dma, dma((OWN_HEADS,)), dma((OWN_HEADS,)), dma, dma, dma, dma,
            dma((OWN_HEADS,)), dma((OWN_HEADS,)), dma, dma, dma,
            pltpu.SemaphoreType.REGULAR,
        ],
        compiler_params=pltpu.CompilerParams(
            collective_id=0, has_side_effects=True, vmem_limit_bytes=56 * 2**20
        ),
        cost_estimate=pl.CostEstimate(
            flops=3_000_000_000, bytes_accessed=8_000_000, transcendentals=6_000_000
        ),
        name="space_time_attention",
    )(proj, q_gain, k_gain, head_weight, steps, timestep, frame_count)


def solution(mesh):
    in_specs = (
        P(("dp", "tm"), None, None, "space", None),
        P("space", None),
        P("space", None),
        P("space", None),
        P(None, "space", None),
        P("dp"),
        P("dp"),
    )
    out_specs = P(("dp", "tm"), "space")
    return jax.shard_map(
        on_device, mesh=mesh, in_specs=in_specs, out_specs=out_specs, check_vma=False
    )
```

```python
import functools
import math

import jax
import jax.numpy as jnp
from jax import lax
from jax.experimental import pallas as pl
from jax.experimental.pallas import tpu as pltpu
from jax.sharding import PartitionSpec as P

HEADS = 40
HEAD = 128
PIXELS = 1024
FRAMES = 16
STEPS = 4
SPACE = 8
OWN_HEADS = HEADS // SPACE
BLOCK = PIXELS // FRAMES
ROWS = PIXELS // 128
QUERY_TILE = 256
GROUP = 8
GROUPS = BLOCK // GROUP
EARLY_HEADS = 3
SIDE = 4
GUEST = OWN_HEADS
PART = 16

EPSILON = 1e-06
CHANNELS = HEADS * HEAD
SCALE_LOG2E = HEAD ** (-0.5) * math.log2(math.e)
MESH = pl.DeviceIdType.MESH


OFFSETS = (
    (2, 2), (2, 3), (2, 1), (3, 2), (1, 2), (2, 0), (0, 2), (3, 1),
    (1, 3), (3, 3), (1, 1), (3, 0), (1, 0), (0, 3), (0, 1),
)


def fold(i):
    return i + i // 2 - 2 * (i // 3)


def space_at(rank):
    return 2 * fold(rank // 2) + rank % 2


def wait_bytes(ref, sem):
    pltpu.make_async_copy(ref, ref, sem).wait()


def column(row):
    return jnp.transpose(jnp.broadcast_to(row, (128, 128)))


def kernel(
    proj, q_gain, k_gain, head_weight, step_scale, timestep, frame_count,
    out,
    x, qk_in, own_qk, o_out, o_in, ssq_out, ssq_in, fac_out, fac_in, normed, fcol, mix, scale, z,
    fin_out, fin_in, gains, weight, steps, head_out, head_in, live, steps_at, counts,
    local_sem, own_sem, qk_send, qk_recv, ssq_send, ssq_recv, fac_send, fac_recv,
    o_send, o_recv, fin_send, fin_recv, last_send, entered, guest_send, head_recv,
):
    me = lax.axis_index("tm")
    sp = lax.axis_index("space")
    dp = lax.axis_index("dp")
    y, xx = me // SIDE, me % SIDE
    down = [jnp.where(y + d >= SIDE, y + d - SIDE, y + d) for d in range(SIDE)]
    along = [jnp.where(xx + d >= SIDE, xx + d - SIDE, xx + d) for d in range(SIDE)]
    peers = [SIDE * down[dy] + along[dx] for dy, dx in OFFSETS]
    half = me % 2

    loads = [
        pltpu.make_async_copy(proj.at[0], x.at[0], local_sem.at[0]),
        pltpu.make_async_copy(proj.at[1], x.at[1], local_sem.at[1]),
        pltpu.make_async_copy(proj.at[2], x.at[2], local_sem.at[2]),
        pltpu.make_async_copy(q_gain, gains.at[0], local_sem.at[3]),
        pltpu.make_async_copy(k_gain, gains.at[1], local_sem.at[4]),
        pltpu.make_async_copy(head_weight, weight, local_sem.at[5]),
        pltpu.make_async_copy(step_scale, steps, local_sem.at[6]),
        pltpu.make_async_copy(timestep, steps_at, local_sem.at[7]),
        pltpu.make_async_copy(frame_count, counts, local_sem.at[8]),
    ]
    for load in loads[:2]:
        load.start()

    barrier = pltpu.get_barrier_semaphore()
    for t in peers:
        pl.semaphore_signal(barrier, inc=1, device_id=(t, sp, dp), device_id_type=MESH)
    rank = 2 * fold(sp // 2) + sp % 2

    late = sp >= SPACE // 2
    partner = 2 * (SPACE // 2 - 1 - sp // 2) + sp % 2
    kinds = [[v + u - jnp.where(v + u >= SIDE, SIDE, 0) for u in along] for v in down]
    kind_of = [kinds[dy][dx] for dy, dx in OFFSETS]
    given = kinds[0][0]

    @pl.when(jnp.logical_not(late))
    def _():
        for t in peers:
            pl.semaphore_signal(
                barrier, inc=1, device_id=(t, partner, dp), device_id_type=MESH
            )

    held = len(peers) + rank + jnp.where(late, len(peers), 0)

    def announce(r, carry):
        pl.semaphore_signal(
            barrier, inc=1, device_id=(me, space_at(r), dp), device_id_type=MESH
        )
        return carry

    lax.fori_loop(rank + 1, SPACE, announce, 0)

    pl.semaphore_wait(barrier, held)

    def enter(r, carry):
        pl.semaphore_signal(
            entered, inc=1, device_id=(me, space_at(r), dp), device_id_type=MESH
        )
        return carry

    def send_ssq(r, carry):
        pltpu.make_async_remote_copy(
            ssq_out, ssq_in.at[sp], ssq_send, ssq_recv,
            device_id=(me, space_at(r), dp), device_id_type=MESH,
        ).start()
        return carry

    def rows_of(t):
        return pl.ds(pl.multiple_of(t * BLOCK, BLOCK), BLOCK)

    def push(source, target, slot, start, size, to, send, recv):
        pltpu.make_async_remote_copy(
            source(start, size), target(slot, start, size), send, recv.at[slot],
            device_id=to, device_id_type=MESH,
        ).start()

    def block_source(ref, h):
        def at(t):
            def rows(start, size):
                first = pl.multiple_of(t * BLOCK + start, PART)
                return ref(h, pl.ds(first, size))

            return rows

        return at

    def qk_target(slot, start, size):
        return qk_in.at[slot, me, :, pl.ds(start, size)]

    def o_target(slot, start, size):
        return o_in.at[slot, me, pl.ds(start, size)]

    def push_main(source, target, h, send, recv):
        for t, kind in zip(peers, kind_of):
            moves = jnp.logical_and(late, kind == h)

            @pl.when(jnp.logical_not(moves))
            def _():
                push(source(t), target, h, 0, BLOCK, (t, sp, dp), send.at[h], recv)

            @pl.when(moves)
            def _():
                push(source(t), target, h, PART, BLOCK - PART, (t, sp, dp), send.at[h], recv)

    def push_moved(source, target, h, send, recv, own_send):
        @pl.when(late)
        def _():
            for t, kind in zip(peers, kind_of):

                @pl.when(kind == h)
                def _():
                    push(source(t), target, GUEST, 0, PART, (t, partner, dp), send.at[h], recv)

            @pl.when(given == h)
            def _():
                push(source(me), target, GUEST, 0, PART, (me, partner, dp), own_send, recv)

    def qk_source(h):
        return block_source(lambda h, rows: proj.at[pl.ds(0, 2), h, rows], h)

    def o_source(h):
        return block_source(lambda h, rows: o_out.at[h, rows], h)

    def send_qk(h):
        push_main(qk_source(h), qk_target, h, qk_send, qk_recv)

    def send_moved_qk(h):
        push_moved(qk_source(h), qk_target, h, qk_send, qk_recv, guest_send.at[0])

    send_qk(0)
    lax.fori_loop(0, rank, enter, 0)
    for load in loads[2:]:
        load.start()

    for c in range(2):
        loads[c].wait()
        for r in range(ROWS):
            total = jnp.zeros((128, 128), jnp.float32)
            for h in range(OWN_HEADS):
                part = x[c, h, 128 * r : 128 * (r + 1), :].astype(jnp.float32)
                total += part * part
            ssq_out[r, c : c + 1, :] = jnp.sum(jnp.transpose(total), axis=0, keepdims=True)
    ssq_in[sp] = ssq_out[...]
    lax.fori_loop(0, rank, send_ssq, 0)

    @pl.when(rank < SPACE // 2)
    def _():
        for h in range(1, EARLY_HEADS):
            send_qk(h)

    @pl.when(rank < SPACE - 1)
    def _():
        pl.semaphore_wait(entered, SPACE - 1 - rank)
        lax.fori_loop(rank + 1, SPACE, send_ssq, 0)

    @pl.when(rank >= SPACE // 2)
    def _():
        send_moved_qk(0)
        for h in range(1, EARLY_HEADS):
            send_qk(h)
            send_moved_qk(h)

    for h in range(EARLY_HEADS, OWN_HEADS - 1):
        send_qk(h)
        send_moved_qk(h)
    own = pltpu.make_async_copy(proj.at[pl.ds(0, 2), :, rows_of(me)], own_qk, own_sem)
    own.start()

    for load in loads[3:]:
        load.wait()
    lane = lax.broadcasted_iota(jnp.int32, (1, 128), 1)
    for b in range(GROUPS):
        row = jnp.zeros((1, 128), jnp.int32)
        for i in range(GROUP):
            row = jnp.where(lane % GROUP == i, counts[me * BLOCK + b * GROUP + i], row)
        live[b : b + 1, :] = row
    for f in range(FRAMES):
        scale[pl.ds(0, OWN_HEADS), f : f + 1, :] = steps[:, pl.ds(steps_at[f], 1), :]

    @pl.when(late)
    def _():
        for c in range(2):
            head_out[c : c + 1, :] = gains[c, pl.ds(given, 1), :]
        for row in range(2, 4):
            head_out[row : row + 1, :] = weight[pl.ds(given, 1), :]
        head_out[4:8, :] = steps[given]
        pltpu.make_async_remote_copy(
            head_out, head_in, guest_send.at[1], head_recv,
            device_id=(me, partner, dp), device_id_type=MESH,
        ).start()

    z[...] = jnp.zeros_like(z)

    wait_bytes(ssq_in.at[pl.ds(0, SPACE - 1)], ssq_recv)
    sums = ssq_in[0]
    for s in range(1, SPACE):
        sums += ssq_in[s]
    fac_out[...] = lax.rsqrt(sums / CHANNELS + EPSILON)
    for t in peers:
        pltpu.make_async_remote_copy(
            fac_out.at[t // 2], fac_in.at[me], fac_send, fac_recv,
            device_id=(t, sp, dp), device_id_type=MESH,
        ).start()
    send_qk(OWN_HEADS - 1)
    fac_in[me] = fac_out[me // 2]

    for c in range(2):
        for r in range(ROWS):
            factor = column(fac_out[r, c : c + 1, :])
            for h in range(OWN_HEADS):
                rows = slice(128 * r, 128 * (r + 1))
                part = x[c, h, rows, :].astype(jnp.float32) * factor
                normed[c, h, rows, :] = (part * gains[c, h : h + 1, :]).astype(jnp.bfloat16)

    loads[2].wait()

    def spatial_head(h, carry):
        def tile(i, carry):
            rows = pl.ds(pl.multiple_of(i * QUERY_TILE, QUERY_TILE), QUERY_TILE)
            scores = lax.dot_general(
                normed[0, h, rows, :], normed[1, h], (((1,), (1,)), ((), ())),
                preferred_element_type=jnp.float32,
            )
            top = jnp.max(scores, axis=1, keepdims=True)
            exponent = jnp.exp2((scores - top) * SCALE_LOG2E)
            share = 1.0 / jnp.sum(exponent, axis=1, keepdims=True)
            weights = (exponent * share).astype(jnp.bfloat16)
            o_out[h, rows, :] = jnp.dot(
                weights, x[2, h], preferred_element_type=jnp.float32
            ).astype(jnp.bfloat16)
            return carry

        lax.fori_loop(0, PIXELS // QUERY_TILE, tile, 0)
        push_main(o_source(h), o_target, h, o_send, o_recv)
        push_moved(o_source(h), o_target, h, o_send, o_recv, guest_send.at[2])
        o_in[h, me] = o_out[h, rows_of(me), :]
        return carry

    lax.fori_loop(0, OWN_HEADS, spatial_head, 0)

    wait_bytes(fac_in.at[pl.ds(0, FRAMES - 1)], fac_recv)
    for c in range(2):
        for f in range(FRAMES):
            fcol[c, f] = column(fac_in[f, c : c + 1, :])
    own.wait()
    for c in range(2):
        for h in range(OWN_HEADS):
            qk_in[h, me, c] = own_qk[c, h]

    @pl.when(late)
    def _():
        qk_in[given, :, :, 0:PART, :] = jnp.zeros((FRAMES, 2, PART, HEAD), jnp.bfloat16)
        o_in[given, :, 0:PART, :] = jnp.zeros((FRAMES, PART, HEAD), jnp.bfloat16)

    @pl.when(jnp.logical_not(late))
    def _():
        rest = BLOCK - PART
        qk_in[GUEST, :, :, PART:BLOCK, :] = jnp.zeros((FRAMES, 2, rest, HEAD), jnp.bfloat16)
        o_in[GUEST, :, PART:BLOCK, :] = jnp.zeros((FRAMES, rest, HEAD), jnp.bfloat16)

    side = FRAMES * GROUP
    at_row = lax.broadcasted_iota(jnp.int32, (side, side), 0)
    at_lane = lax.broadcasted_iota(jnp.int32, (side, side), 1)
    same = (at_row % GROUP) == (at_lane % GROUP)
    key_frame = at_lane // GROUP
    my_half = pl.ds(pl.multiple_of(half * BLOCK, BLOCK), BLOCK)

    heads = OWN_HEADS + jnp.where(late, 0, 1)

    @pl.when(jnp.logical_not(late))
    def _():
        wait_bytes(head_in, head_recv)
        for f in range(FRAMES):
            scale[GUEST, f : f + 1, :] = head_in[pl.ds(4 + steps_at[f], 1), :]

    def arrive(part, sems, h):
        less = jnp.logical_and(late, given == h)

        @pl.when(jnp.logical_and(h < GUEST, jnp.logical_not(less)))
        def _():
            wait_bytes(part(h, FRAMES - 1, BLOCK), sems.at[h])

        @pl.when(less)
        def _():
            wait_bytes(part(h, FRAMES - 1, BLOCK - PART), sems.at[h])

        @pl.when(h == GUEST)
        def _():
            wait_bytes(part(h, FRAMES, PART), sems.at[h])

    def qk_part(h, frames, rows):
        return qk_in.at[h, pl.ds(0, frames), :, pl.ds(0, rows)]

    def o_part(h, frames, rows):
        return o_in.at[h, pl.ds(0, frames), pl.ds(0, rows)]

    def of_head(own, row, h):
        return jnp.where(h < GUEST, own[pl.ds(jnp.minimum(h, GUEST - 1), 1), :], row)

    def temporal_weights(h, carry):
        arrive(qk_part, qk_recv, h)
        wide = []
        for c in range(2):
            part = qk_in[h, :, c].astype(jnp.float32) * fcol[c, :, my_half, :]
            gain = of_head(gains.at[c], head_in[c : c + 1, :], h)
            wide.append(part * gain.reshape(1, 1, HEAD))
        for b in range(GROUPS):
            queries, keys = (
                w[:, GROUP * b : GROUP * (b + 1), :].reshape(side, HEAD).astype(jnp.bfloat16)
                for w in wide
            )
            scores = lax.dot_general(
                queries, keys, (((1,), (1,)), ((), ())), preferred_element_type=jnp.float32
            )
            seen = same & (key_frame < live[b : b + 1, :])
            scores = jnp.where(seen, scores, -1e30)
            top = jnp.max(scores, axis=1, keepdims=True)
            exponent = jnp.exp2((scores - top) * SCALE_LOG2E)
            share = 1.0 / jnp.sum(exponent, axis=1, keepdims=True)
            mix[h, b] = (exponent * share).astype(jnp.bfloat16)
        return carry

    lax.fori_loop(0, heads, temporal_weights, 0)

    at_frame = lax.broadcasted_iota(jnp.int32, (FRAMES, GROUP, 128), 0)
    at_lane3 = lax.broadcasted_iota(jnp.int32, (FRAMES, GROUP, 128), 2)
    dot_lane = at_frame == at_lane3
    square_lane = at_frame + FRAMES == at_lane3

    def temporal_head(h, carry):
        arrive(o_part, o_recv, h)
        spatial = o_in[h].astype(jnp.float32)
        row_scale = scale[h].reshape(FRAMES, 1, HEAD)
        row_weight = of_head(weight, head_in[2:3, :], h).reshape(1, 1, HEAD)
        for b in range(GROUPS):
            pixels = slice(GROUP * b, GROUP * (b + 1))
            block = spatial[:, pixels, :]
            mixed = jnp.dot(
                mix[h, b], block.reshape(side, HEAD).astype(jnp.bfloat16),
                preferred_element_type=jnp.float32,
            ).astype(jnp.bfloat16).astype(jnp.float32)
            modulated = (block + mixed.reshape(FRAMES, GROUP, HEAD)) * row_scale
            dots = jnp.sum(modulated * row_weight, axis=2, keepdims=True)
            squares = jnp.sum(modulated * modulated, axis=2, keepdims=True)
            placed = jnp.where(dot_lane, dots, 0.0) + jnp.where(square_lane, squares, 0.0)
            at = pl.ds(pl.multiple_of(half * BLOCK + GROUP * b, GROUP), GROUP)
            z[at, :] += jnp.sum(placed, axis=0)
        return carry

    lax.fori_loop(0, heads, temporal_head, 0)

    turned = jnp.transpose(z[...])
    for f in range(FRAMES):
        fin_out[f, 0:1, :] = turned[f : f + 1, :]
        fin_out[f, 1:2, :] = turned[FRAMES + f : FRAMES + f + 1, :]
    owner = me // 2
    slot = half * SPACE + sp
    for t in peers:
        pltpu.make_async_remote_copy(
            fin_out.at[t], fin_in.at[slot], fin_send, fin_recv,
            device_id=(t, owner, dp), device_id_type=MESH,
        ).start()

    @pl.when(sp == owner)
    def _():
        here = pltpu.make_async_copy(fin_out.at[me], fin_in.at[slot], fin_recv)
        here.start()

    @pl.when(sp != owner)
    def _():
        away = pltpu.make_async_remote_copy(
            fin_out.at[me], fin_in.at[slot], last_send, fin_recv,
            device_id=(me, owner, dp), device_id_type=MESH,
        )
        away.start()
        away.wait_send()

    wait_bytes(ssq_in.at[pl.ds(0, SPACE - 1)], ssq_send)
    wait_bytes(fac_in.at[pl.ds(0, FRAMES - 1)], fac_send)
    for h in range(OWN_HEADS):
        wait_bytes(qk_in.at[h, pl.ds(0, FRAMES - 1)], qk_send.at[h])
        wait_bytes(o_in.at[h, pl.ds(0, FRAMES - 1)], o_send.at[h])

    @pl.when(late)
    def _():
        wait_bytes(qk_part(GUEST, 1, PART), guest_send.at[0])
        wait_bytes(head_out, guest_send.at[1])
        wait_bytes(o_part(GUEST, 1, PART), guest_send.at[2])

    wait_bytes(fin_out.at[pl.ds(0, FRAMES - 1)], fin_send)
    wait_bytes(fin_in, fin_recv)
    out[...] = jnp.sum(fin_in[...], axis=0)


def on_device(projected, q_gain, k_gain, head_weight, step_scale, timestep, frame_count):
    proj = jnp.transpose(projected[0], (1, 2, 0, 3))
    steps = jnp.transpose(step_scale, (1, 0, 2))
    any_space = pl.BlockSpec(memory_space=pl.ANY)
    bf16, f32 = jnp.bfloat16, jnp.float32
    dma = pltpu.SemaphoreType.DMA
    totals = pl.pallas_call(
        kernel,
        out_shape=jax.ShapeDtypeStruct((2, 128), f32),
        in_specs=[any_space] * 7,
        out_specs=pl.BlockSpec(memory_space=pltpu.VMEM),
        scratch_shapes=[
            pltpu.VMEM((3, OWN_HEADS, PIXELS, HEAD), bf16),
            pltpu.VMEM((OWN_HEADS + 1, FRAMES, 2, BLOCK, HEAD), bf16),
            pltpu.VMEM((2, OWN_HEADS, BLOCK, HEAD), bf16),
            pltpu.VMEM((OWN_HEADS, PIXELS, HEAD), bf16),
            pltpu.VMEM((OWN_HEADS + 1, FRAMES, BLOCK, HEAD), bf16),
            pltpu.VMEM((ROWS, 2, 128), f32),
            pltpu.VMEM((SPACE, ROWS, 2, 128), f32),
            pltpu.VMEM((ROWS, 2, 128), f32),
            pltpu.VMEM((FRAMES, 2, 128), f32),
            pltpu.VMEM((2, OWN_HEADS, PIXELS, HEAD), bf16),
            pltpu.VMEM((2, FRAMES, 128, 128), f32),
            pltpu.VMEM((OWN_HEADS + 1, GROUPS, 128, 128), bf16),
            pltpu.VMEM((OWN_HEADS + 1, FRAMES, HEAD), f32),
            pltpu.VMEM((128, 128), f32),
            pltpu.VMEM((FRAMES, 2, 128), f32),
            pltpu.VMEM((FRAMES, 2, 128), f32),
            pltpu.VMEM((2, OWN_HEADS, HEAD), f32),
            pltpu.VMEM((OWN_HEADS, HEAD), f32),
            pltpu.VMEM((OWN_HEADS, STEPS, HEAD), f32),
            pltpu.VMEM((8, HEAD), f32),
            pltpu.VMEM((8, HEAD), f32),
            pltpu.VMEM((GROUPS, 128), jnp.int32),
            pltpu.SMEM((FRAMES,), jnp.int32),
            pltpu.SMEM((PIXELS,), jnp.int32),
            dma((9,)), dma, dma((OWN_HEADS,)), dma((OWN_HEADS + 1,)), dma, dma, dma, dma,
            dma((OWN_HEADS,)), dma((OWN_HEADS + 1,)), dma, dma, dma,
            pltpu.SemaphoreType.REGULAR, dma((3,)), dma,
        ],
        compiler_params=pltpu.CompilerParams(
            collective_id=0, has_side_effects=True, vmem_limit_bytes=56 * 2**20
        ),
        cost_estimate=pl.CostEstimate(
            flops=3_000_000_000, bytes_accessed=8_000_000, transcendentals=6_000_000
        ),
        name="space_time_attention",
    )(proj, q_gain, k_gain, head_weight, steps, timestep, frame_count)
    return totals[0:1] * lax.rsqrt(totals[1:2] / CHANNELS + EPSILON)


def solution(mesh):
    in_specs = (
        P(("dp", "tm"), None, None, "space", None),
        P("space", None),
        P("space", None),
        P("space", None),
        P(None, "space", None),
        P("dp"),
        P("dp"),
    )
    out_specs = P(("dp", "tm"), "space")
    return jax.shard_map(
        on_device, mesh=mesh, in_specs=in_specs, out_specs=out_specs, check_vma=False
    )
```

```python
import functools
import math

import jax
import jax.numpy as jnp
from jax import lax
from jax.experimental import pallas as pl
from jax.experimental.pallas import tpu as pltpu
from jax.sharding import PartitionSpec as P

HEADS = 40
HEAD = 128
PIXELS = 1024
FRAMES = 16
STEPS = 4
SPACE = 8
OWN_HEADS = HEADS // SPACE
BLOCK = PIXELS // FRAMES
ROWS = PIXELS // 128
QUERY_TILE = 256
GROUP = 8
GROUPS = BLOCK // GROUP
EARLY_HEADS = 3
SIDE = 4
GUEST = OWN_HEADS
SLOTS = OWN_HEADS + 2
PART = 16

EPSILON = 1e-06
CHANNELS = HEADS * HEAD
SCALE_LOG2E = HEAD ** (-0.5) * math.log2(math.e)
MESH = pl.DeviceIdType.MESH


OFFSETS = (
    (2, 2), (2, 3), (2, 1), (3, 2), (1, 2), (2, 0), (0, 2), (3, 1),
    (1, 3), (3, 3), (1, 1), (3, 0), (1, 0), (0, 3), (0, 1),
)


def wait_bytes(ref, sem):
    pltpu.make_async_copy(ref, ref, sem).wait()


def column(row):
    return jnp.transpose(jnp.broadcast_to(row, (128, 128)))


def kernel(
    proj, q_gain, k_gain, head_weight, step_scale, timestep, frame_count,
    out,
    x, qk_in, own_qk, o_out, o_in, ssq_out, ssq_in, fac_out, fac_in, normed, fcol, mix, scale, z,
    fin_out, fin_in, gains, weight, steps, head_out, head_in, live, steps_at, counts,
    local_sem, own_sem, qk_send, qk_recv, ssq_send, ssq_recv, fac_send, fac_recv,
    o_send, o_recv, fin_send, fin_recv, last_send, entered, guest_qk_send, guest_o_send, head_send, head_recv,
):
    me = lax.axis_index("tm")
    sp = lax.axis_index("space")
    dp = lax.axis_index("dp")
    y, xx = me // SIDE, me % SIDE
    down = [jnp.where(y + d >= SIDE, y + d - SIDE, y + d) for d in range(SIDE)]
    along = [jnp.where(xx + d >= SIDE, xx + d - SIDE, xx + d) for d in range(SIDE)]
    peers = [SIDE * down[dy] + along[dx] for dy, dx in OFFSETS]
    half = me % 2

    loads = [
        pltpu.make_async_copy(proj.at[0], x.at[0], local_sem.at[0]),
        pltpu.make_async_copy(proj.at[1], x.at[1], local_sem.at[1]),
        pltpu.make_async_copy(proj.at[2], x.at[2], local_sem.at[2]),
        pltpu.make_async_copy(q_gain, gains.at[0], local_sem.at[3]),
        pltpu.make_async_copy(k_gain, gains.at[1], local_sem.at[4]),
        pltpu.make_async_copy(head_weight, weight, local_sem.at[5]),
        pltpu.make_async_copy(step_scale, steps, local_sem.at[6]),
        pltpu.make_async_copy(timestep, steps_at, local_sem.at[7]),
        pltpu.make_async_copy(frame_count, counts, local_sem.at[8]),
    ]
    for load in loads[:2]:
        load.start()

    barrier = pltpu.get_barrier_semaphore()
    for t in peers:
        pl.semaphore_signal(barrier, inc=1, device_id=(t, sp, dp), device_id_type=MESH)
    rank = sp

    kinds = [[v + u - jnp.where(v + u >= SIDE, SIDE, 0) for u in along] for v in down]
    kind_of = [kinds[dy][dx] for dy, dx in OFFSETS]
    kind = kinds[0][0]
    late = sp >= SPACE // 2
    last = jnp.logical_and(late, sp < SPACE // 2 + 2)
    partner = 2 * (SPACE // 2 - 1 - sp // 2) + sp % 2

    def next_head(k):
        return k + 1 - jnp.where(k == SIDE - 1, SIDE, 0)

    gifts = (
        (late, partner, lambda k: k, lambda k: k >= 0, GUEST),
        (last, sp % 2, next_head, lambda k: k % 2 == 0, GUEST + 1),
    )
    first_host = jnp.logical_not(late)
    second_host = jnp.logical_and(sp < 2, kind % 2 == 0)

    @pl.when(first_host)
    def _():
        for t in peers:
            pl.semaphore_signal(
                barrier, inc=1, device_id=(t, partner, dp), device_id_type=MESH
            )

    @pl.when(second_host)
    def _():
        for t in peers:
            pl.semaphore_signal(
                barrier, inc=1, device_id=(t, sp + SPACE // 2, dp), device_id_type=MESH
            )

    held = len(peers) + rank + jnp.where(late, len(peers), 0)
    held += jnp.where(last, FRAMES // 2 - jnp.where(kind % 2 == 0, 1, 0), 0)

    def announce(r, carry):
        pl.semaphore_signal(
            barrier, inc=1, device_id=(me, r, dp), device_id_type=MESH
        )
        return carry

    lax.fori_loop(rank + 1, SPACE, announce, 0)

    pl.semaphore_wait(barrier, held)

    def enter(r, carry):
        pl.semaphore_signal(
            entered, inc=1, device_id=(me, r, dp), device_id_type=MESH
        )
        return carry

    def send_ssq(r, carry):
        pltpu.make_async_remote_copy(
            ssq_out, ssq_in.at[sp], ssq_send, ssq_recv,
            device_id=(me, r, dp), device_id_type=MESH,
        ).start()
        return carry

    def rows_of(t):
        return pl.ds(pl.multiple_of(t * BLOCK, BLOCK), BLOCK)

    def push(source, target, slot, start, size, to, send, recv):
        pltpu.make_async_remote_copy(
            source(start, size), target(slot, start, size), send, recv.at[slot],
            device_id=to, device_id_type=MESH,
        ).start()

    def block_source(ref, h):
        def at(t):
            def rows(start, size):
                first = pl.multiple_of(t * BLOCK + start, PART)
                return ref(h, pl.ds(first, size))

            return rows

        return at

    def qk_target(slot, start, size):
        return qk_in.at[slot, me, :, pl.ds(start, size)]

    def o_target(slot, start, size):
        return o_in.at[slot, me, pl.ds(start, size)]

    def moves(h, k):
        made = [
            jnp.logical_and(gives, jnp.logical_and(has(k), head(k) == h))
            for gives, _, head, has, _ in gifts
        ]
        return jnp.logical_or(made[0], made[1])

    def push_main(source, target, h, send, recv):
        for t, k in zip(peers, kind_of):

            @pl.when(jnp.logical_not(moves(h, k)))
            def _():
                push(source(t), target, h, 0, BLOCK, (t, sp, dp), send.at[h], recv)

            @pl.when(moves(h, k))
            def _():
                push(source(t), target, h, PART, BLOCK - PART, (t, sp, dp), send.at[h], recv)

    def push_moved(source, target, h, send, recv, own_send):
        for gives, plane, head, has, slot in gifts:

            @pl.when(gives)
            def _():
                for t, k in zip(peers, kind_of):

                    @pl.when(jnp.logical_and(has(k), head(k) == h))
                    def _():
                        push(source(t), target, slot, 0, PART, (t, plane, dp), send.at[h], recv)

                @pl.when(jnp.logical_and(has(kind), head(kind) == h))
                def _():
                    push(
                        source(me), target, slot, 0, PART, (me, plane, dp),
                        own_send.at[slot - GUEST], recv,
                    )

    def qk_source(h):
        return block_source(lambda h, rows: proj.at[pl.ds(0, 2), h, rows], h)

    def o_source(h):
        return block_source(lambda h, rows: o_out.at[h, rows], h)

    def send_qk(h):
        push_main(qk_source(h), qk_target, h, qk_send, qk_recv)

    def send_moved_qk(h):
        push_moved(qk_source(h), qk_target, h, qk_send, qk_recv, guest_qk_send)

    send_qk(0)
    lax.fori_loop(0, rank, enter, 0)
    for load in loads[2:]:
        load.start()

    for c in range(2):
        loads[c].wait()
        for r in range(ROWS):
            total = jnp.zeros((128, 128), jnp.float32)
            for h in range(OWN_HEADS):
                part = x[c, h, 128 * r : 128 * (r + 1), :].astype(jnp.float32)
                total += part * part
            ssq_out[r, c : c + 1, :] = jnp.sum(jnp.transpose(total), axis=0, keepdims=True)
    ssq_in[sp] = ssq_out[...]
    lax.fori_loop(0, rank, send_ssq, 0)

    @pl.when(rank < SPACE // 2)
    def _():
        for h in range(1, EARLY_HEADS):
            send_qk(h)

    @pl.when(rank < SPACE - 1)
    def _():
        pl.semaphore_wait(entered, SPACE - 1 - rank)
        lax.fori_loop(rank + 1, SPACE, send_ssq, 0)

    @pl.when(rank >= SPACE // 2)
    def _():
        send_moved_qk(0)
        for h in range(1, EARLY_HEADS):
            send_qk(h)
            send_moved_qk(h)

    for h in range(EARLY_HEADS, OWN_HEADS - 1):
        send_qk(h)
        send_moved_qk(h)
    own = pltpu.make_async_copy(proj.at[pl.ds(0, 2), :, rows_of(me)], own_qk, own_sem)
    own.start()

    for load in loads[3:]:
        load.wait()
    lane = lax.broadcasted_iota(jnp.int32, (1, 128), 1)
    for b in range(GROUPS):
        row = jnp.zeros((1, 128), jnp.int32)
        for i in range(GROUP):
            row = jnp.where(lane % GROUP == i, counts[me * BLOCK + b * GROUP + i], row)
        live[b : b + 1, :] = row
    for f in range(FRAMES):
        scale[pl.ds(0, OWN_HEADS), f : f + 1, :] = steps[:, pl.ds(steps_at[f], 1), :]

    for gives, plane, head, has, slot in gifts:
        guest = slot - GUEST

        @pl.when(jnp.logical_and(gives, has(kind)))
        def _():
            row = pl.ds(head(kind), 1)
            for c in range(2):
                head_out[guest, c : c + 1, :] = gains[c, row, :]
            for c in range(2, 4):
                head_out[guest, c : c + 1, :] = weight[row, :]
            head_out[guest, 4:8, :] = steps[head(kind)]
            pltpu.make_async_remote_copy(
                head_out.at[guest], head_in.at[guest], head_send.at[guest], head_recv.at[guest],
                device_id=(me, plane, dp), device_id_type=MESH,
            ).start()

    z[...] = jnp.zeros_like(z)

    wait_bytes(ssq_in.at[pl.ds(0, SPACE - 1)], ssq_recv)
    sums = ssq_in[0]
    for s in range(1, SPACE):
        sums += ssq_in[s]
    fac_out[...] = lax.rsqrt(sums / CHANNELS + EPSILON)
    for t in peers:
        pltpu.make_async_remote_copy(
            fac_out.at[t // 2], fac_in.at[me], fac_send, fac_recv,
            device_id=(t, sp, dp), device_id_type=MESH,
        ).start()
    send_qk(OWN_HEADS - 1)
    fac_in[me] = fac_out[me // 2]

    for c in range(2):
        for r in range(ROWS):
            factor = column(fac_out[r, c : c + 1, :])
            for h in range(OWN_HEADS):
                rows = slice(128 * r, 128 * (r + 1))
                part = x[c, h, rows, :].astype(jnp.float32) * factor
                normed[c, h, rows, :] = (part * gains[c, h : h + 1, :]).astype(jnp.bfloat16)

    loads[2].wait()

    def spatial_head(h, carry):
        def tile(i, carry):
            rows = pl.ds(pl.multiple_of(i * QUERY_TILE, QUERY_TILE), QUERY_TILE)
            scores = lax.dot_general(
                normed[0, h, rows, :], normed[1, h], (((1,), (1,)), ((), ())),
                preferred_element_type=jnp.float32,
            )
            top = jnp.max(scores, axis=1, keepdims=True)
            exponent = jnp.exp2((scores - top) * SCALE_LOG2E)
            share = 1.0 / jnp.sum(exponent, axis=1, keepdims=True)
            weights = (exponent * share).astype(jnp.bfloat16)
            o_out[h, rows, :] = jnp.dot(
                weights, x[2, h], preferred_element_type=jnp.float32
            ).astype(jnp.bfloat16)
            return carry

        lax.fori_loop(0, PIXELS // QUERY_TILE, tile, 0)
        push_main(o_source(h), o_target, h, o_send, o_recv)
        push_moved(o_source(h), o_target, h, o_send, o_recv, guest_o_send)
        o_in[h, me] = o_out[h, rows_of(me), :]
        return carry

    lax.fori_loop(0, OWN_HEADS, spatial_head, 0)

    wait_bytes(fac_in.at[pl.ds(0, FRAMES - 1)], fac_recv)
    for c in range(2):
        for f in range(FRAMES):
            fcol[c, f] = column(fac_in[f, c : c + 1, :])
    own.wait()
    for c in range(2):
        for h in range(OWN_HEADS):
            qk_in[h, me, c] = own_qk[c, h]

    for gives, _, head, has, _ in gifts:

        @pl.when(jnp.logical_and(gives, has(kind)))
        def _():
            none = jnp.zeros((FRAMES, PART, HEAD), jnp.bfloat16)
            for c in range(2):
                qk_in[head(kind), :, c, 0:PART, :] = none
            o_in[head(kind), :, 0:PART, :] = none

    for hosts, slot in ((first_host, GUEST), (second_host, GUEST + 1)):

        @pl.when(hosts)
        def _():
            none = jnp.zeros((FRAMES, BLOCK - PART, HEAD), jnp.bfloat16)
            for c in range(2):
                qk_in[slot, :, c, PART:BLOCK, :] = none
            o_in[slot, :, PART:BLOCK, :] = none
            wait_bytes(head_in.at[slot - GUEST], head_recv.at[slot - GUEST])

    for hosts, slot in ((first_host, GUEST), (second_host, GUEST + 1)):

        @pl.when(hosts)
        def _():
            for f in range(FRAMES):
                row = head_in[slot - GUEST, pl.ds(4 + steps_at[f], 1), :]
                scale[slot, f : f + 1, :] = row

    side = FRAMES * GROUP
    at_row = lax.broadcasted_iota(jnp.int32, (side, side), 0)
    at_lane = lax.broadcasted_iota(jnp.int32, (side, side), 1)
    same = (at_row % GROUP) == (at_lane % GROUP)
    key_frame = at_lane // GROUP
    my_half = pl.ds(pl.multiple_of(half * BLOCK, BLOCK), BLOCK)

    heads = OWN_HEADS + jnp.where(first_host, 1, 0) + jnp.where(second_host, 1, 0)

    def arrive(part, sems, h):
        less = moves(h, kind)

        @pl.when(jnp.logical_and(h < GUEST, jnp.logical_not(less)))
        def _():
            wait_bytes(part(h, FRAMES - 1, BLOCK), sems.at[h])

        @pl.when(less)
        def _():
            wait_bytes(part(h, FRAMES - 1, BLOCK - PART), sems.at[h])

        @pl.when(h >= GUEST)
        def _():
            wait_bytes(part(h, FRAMES, PART), sems.at[h])

    def qk_part(h, frames, rows):
        return qk_in.at[h, pl.ds(0, frames), :, pl.ds(0, rows)]

    def o_part(h, frames, rows):
        return o_in.at[h, pl.ds(0, frames), pl.ds(0, rows)]

    def of_head(own, row, h):
        guest = head_in[jnp.maximum(h - GUEST, 0), row : row + 1, :]
        return jnp.where(h < GUEST, own[pl.ds(jnp.minimum(h, GUEST - 1), 1), :], guest)

    def temporal_weights(h, carry):
        arrive(qk_part, qk_recv, h)
        wide = []
        for c in range(2):
            part = qk_in[h, :, c].astype(jnp.float32) * fcol[c, :, my_half, :]
            gain = of_head(gains.at[c], c, h)
            wide.append(part * gain.reshape(1, 1, HEAD))
        for b in range(GROUPS):
            queries, keys = (
                w[:, GROUP * b : GROUP * (b + 1), :].reshape(side, HEAD).astype(jnp.bfloat16)
                for w in wide
            )
            scores = lax.dot_general(
                queries, keys, (((1,), (1,)), ((), ())), preferred_element_type=jnp.float32
            )
            seen = same & (key_frame < live[b : b + 1, :])
            scores = jnp.where(seen, scores, -1e30)
            top = jnp.max(scores, axis=1, keepdims=True)
            exponent = jnp.exp2((scores - top) * SCALE_LOG2E)
            share = 1.0 / jnp.sum(exponent, axis=1, keepdims=True)
            mix[h, b] = (exponent * share).astype(jnp.bfloat16)
        return carry

    lax.fori_loop(0, heads, temporal_weights, 0)

    at_frame = lax.broadcasted_iota(jnp.int32, (FRAMES, GROUP, 128), 0)
    at_lane3 = lax.broadcasted_iota(jnp.int32, (FRAMES, GROUP, 128), 2)
    dot_lane = at_frame == at_lane3
    square_lane = at_frame + FRAMES == at_lane3

    def temporal_head(h, carry):
        arrive(o_part, o_recv, h)
        spatial = o_in[h].astype(jnp.float32)
        row_scale = scale[h].reshape(FRAMES, 1, HEAD)
        row_weight = of_head(weight, 2, h).reshape(1, 1, HEAD)
        for b in range(GROUPS):
            pixels = slice(GROUP * b, GROUP * (b + 1))
            block = spatial[:, pixels, :]
            mixed = jnp.dot(
                mix[h, b], block.reshape(side, HEAD).astype(jnp.bfloat16),
                preferred_element_type=jnp.float32,
            ).astype(jnp.bfloat16).astype(jnp.float32)
            modulated = (block + mixed.reshape(FRAMES, GROUP, HEAD)) * row_scale
            dots = jnp.sum(modulated * row_weight, axis=2, keepdims=True)
            squares = jnp.sum(modulated * modulated, axis=2, keepdims=True)
            placed = jnp.where(dot_lane, dots, 0.0) + jnp.where(square_lane, squares, 0.0)
            at = pl.ds(pl.multiple_of(half * BLOCK + GROUP * b, GROUP), GROUP)
            z[at, :] += jnp.sum(placed, axis=0)
        return carry

    lax.fori_loop(0, heads, temporal_head, 0)

    turned = jnp.transpose(z[...])
    for f in range(FRAMES):
        fin_out[f, 0:1, :] = turned[f : f + 1, :]
        fin_out[f, 1:2, :] = turned[FRAMES + f : FRAMES + f + 1, :]
    owner = me // 2
    slot = half * SPACE + sp
    for t in peers:
        pltpu.make_async_remote_copy(
            fin_out.at[t], fin_in.at[slot], fin_send, fin_recv,
            device_id=(t, owner, dp), device_id_type=MESH,
        ).start()

    @pl.when(sp == owner)
    def _():
        here = pltpu.make_async_copy(fin_out.at[me], fin_in.at[slot], fin_recv)
        here.start()

    @pl.when(sp != owner)
    def _():
        away = pltpu.make_async_remote_copy(
            fin_out.at[me], fin_in.at[slot], last_send, fin_recv,
            device_id=(me, owner, dp), device_id_type=MESH,
        )
        away.start()
        away.wait_send()

    wait_bytes(ssq_in.at[pl.ds(0, SPACE - 1)], ssq_send)
    wait_bytes(fac_in.at[pl.ds(0, FRAMES - 1)], fac_send)
    for h in range(OWN_HEADS):
        wait_bytes(qk_in.at[h, pl.ds(0, FRAMES - 1)], qk_send.at[h])
        wait_bytes(o_in.at[h, pl.ds(0, FRAMES - 1)], o_send.at[h])

    for gives, _, _, has, slot in gifts:
        guest = slot - GUEST

        @pl.when(jnp.logical_and(gives, has(kind)))
        def _():
            wait_bytes(qk_part(slot, 1, PART), guest_qk_send.at[guest])
            wait_bytes(head_out.at[guest], head_send.at[guest])
            wait_bytes(o_part(slot, 1, PART), guest_o_send.at[guest])

    wait_bytes(fin_out.at[pl.ds(0, FRAMES - 1)], fin_send)
    wait_bytes(fin_in, fin_recv)
    totals = jnp.sum(fin_in[...], axis=0)
    out[...] = totals[0:1, :] * lax.rsqrt(totals[1:2, :] / CHANNELS + EPSILON)


def on_device(projected, q_gain, k_gain, head_weight, step_scale, timestep, frame_count):
    proj = jnp.transpose(projected[0], (1, 2, 0, 3))
    steps = jnp.transpose(step_scale, (1, 0, 2))
    any_space = pl.BlockSpec(memory_space=pl.ANY)
    bf16, f32 = jnp.bfloat16, jnp.float32
    dma = pltpu.SemaphoreType.DMA
    return pl.pallas_call(
        kernel,
        out_shape=jax.ShapeDtypeStruct((1, 128), f32),
        in_specs=[any_space] * 7,
        out_specs=pl.BlockSpec(memory_space=pltpu.VMEM),
        scratch_shapes=[
            pltpu.VMEM((3, OWN_HEADS, PIXELS, HEAD), bf16),
            pltpu.VMEM((SLOTS, FRAMES, 2, BLOCK, HEAD), bf16),
            pltpu.VMEM((2, OWN_HEADS, BLOCK, HEAD), bf16),
            pltpu.VMEM((OWN_HEADS, PIXELS, HEAD), bf16),
            pltpu.VMEM((SLOTS, FRAMES, BLOCK, HEAD), bf16),
            pltpu.VMEM((ROWS, 2, 128), f32),
            pltpu.VMEM((SPACE, ROWS, 2, 128), f32),
            pltpu.VMEM((ROWS, 2, 128), f32),
            pltpu.VMEM((FRAMES, 2, 128), f32),
            pltpu.VMEM((2, OWN_HEADS, PIXELS, HEAD), bf16),
            pltpu.VMEM((2, FRAMES, 128, 128), f32),
            pltpu.VMEM((SLOTS, GROUPS, 128, 128), bf16),
            pltpu.VMEM((SLOTS, FRAMES, HEAD), f32),
            pltpu.VMEM((128, 128), f32),
            pltpu.VMEM((FRAMES, 2, 128), f32),
            pltpu.VMEM((FRAMES, 2, 128), f32),
            pltpu.VMEM((2, OWN_HEADS, HEAD), f32),
            pltpu.VMEM((OWN_HEADS, HEAD), f32),
            pltpu.VMEM((OWN_HEADS, STEPS, HEAD), f32),
            pltpu.VMEM((2, 8, HEAD), f32),
            pltpu.VMEM((2, 8, HEAD), f32),
            pltpu.VMEM((GROUPS, 128), jnp.int32),
            pltpu.SMEM((FRAMES,), jnp.int32),
            pltpu.SMEM((PIXELS,), jnp.int32),
            dma((9,)), dma, dma((OWN_HEADS,)), dma((SLOTS,)), dma, dma, dma, dma,
            dma((OWN_HEADS,)), dma((SLOTS,)), dma, dma, dma,
            pltpu.SemaphoreType.REGULAR, dma((2,)), dma((2,)), dma((2,)), dma((2,)),
        ],
        compiler_params=pltpu.CompilerParams(
            collective_id=0, has_side_effects=True, vmem_limit_bytes=56 * 2**20
        ),
        cost_estimate=pl.CostEstimate(
            flops=3_000_000_000, bytes_accessed=8_000_000, transcendentals=6_000_000
        ),
        name="space_time_attention",
    )(proj, q_gain, k_gain, head_weight, steps, timestep, frame_count)


def solution(mesh):
    in_specs = (
        P(("dp", "tm"), None, None, "space", None),
        P("space", None),
        P("space", None),
        P("space", None),
        P(None, "space", None),
        P("dp"),
        P("dp"),
    )
    out_specs = P(("dp", "tm"), "space")
    return jax.shard_map(
        on_device, mesh=mesh, in_specs=in_specs, out_specs=out_specs, check_vma=False
    )
```

```python
import functools
import math

import jax
import jax.numpy as jnp
from jax import lax
from jax.experimental import pallas as pl
from jax.experimental.pallas import tpu as pltpu
from jax.sharding import PartitionSpec as P

HEADS = 40
HEAD = 128
PIXELS = 1024
FRAMES = 16
STEPS = 4
SPACE = 8
OWN_HEADS = HEADS // SPACE
BLOCK = PIXELS // FRAMES
ROWS = PIXELS // 128
QUERY_TILE = 256
GROUP = 8
GROUPS = BLOCK // GROUP
EARLY_HEADS = 3
SIDE = 4
GUEST = OWN_HEADS
SLOTS = OWN_HEADS + 2
LAST_PLANE = 4
SECOND_HOST = 1
PART = 16

EPSILON = 1e-06
CHANNELS = HEADS * HEAD
SCALE_LOG2E = HEAD ** (-0.5) * math.log2(math.e)
MESH = pl.DeviceIdType.MESH


OFFSETS = (
    (2, 2), (2, 3), (2, 1), (3, 2), (1, 2), (2, 0), (0, 2), (3, 1),
    (1, 3), (3, 3), (1, 1), (3, 0), (1, 0), (0, 3), (0, 1),
)


def wait_bytes(ref, sem):
    pltpu.make_async_copy(ref, ref, sem).wait()


def column(row):
    return jnp.transpose(jnp.broadcast_to(row, (128, 128)))


def kernel(
    proj, q_gain, k_gain, head_weight, step_scale, timestep, frame_count,
    out,
    x, qk_in, own_qk, o_out, o_in, ssq_out, ssq_in, fac_out, fac_in, normed, fcol, mix, scale, z,
    fin_out, fin_in, gains, weight, steps, head_out, head_in, live, steps_at, counts,
    local_sem, own_sem, qk_send, qk_recv, ssq_send, ssq_recv, fac_send, fac_recv,
    o_send, o_recv, fin_send, fin_recv, last_send, entered, guest_qk_send, guest_o_send, head_send, head_recv,
):
    me = lax.axis_index("tm")
    sp = lax.axis_index("space")
    dp = lax.axis_index("dp")
    y, xx = me // SIDE, me % SIDE
    down = [jnp.where(y + d >= SIDE, y + d - SIDE, y + d) for d in range(SIDE)]
    along = [jnp.where(xx + d >= SIDE, xx + d - SIDE, xx + d) for d in range(SIDE)]
    peers = [SIDE * down[dy] + along[dx] for dy, dx in OFFSETS]
    half = me % 2

    loads = [
        pltpu.make_async_copy(proj.at[0], x.at[0], local_sem.at[0]),
        pltpu.make_async_copy(proj.at[1], x.at[1], local_sem.at[1]),
        pltpu.make_async_copy(proj.at[2], x.at[2], local_sem.at[2]),
        pltpu.make_async_copy(q_gain, gains.at[0], local_sem.at[3]),
        pltpu.make_async_copy(k_gain, gains.at[1], local_sem.at[4]),
        pltpu.make_async_copy(head_weight, weight, local_sem.at[5]),
        pltpu.make_async_copy(step_scale, steps, local_sem.at[6]),
        pltpu.make_async_copy(timestep, steps_at, local_sem.at[7]),
        pltpu.make_async_copy(frame_count, counts, local_sem.at[8]),
    ]
    for load in loads[:2]:
        load.start()

    barrier = pltpu.get_barrier_semaphore()
    for t in peers:
        pl.semaphore_signal(barrier, inc=1, device_id=(t, sp, dp), device_id_type=MESH)
    rank = sp

    kinds = [[v + u - jnp.where(v + u >= SIDE, SIDE, 0) for u in along] for v in down]
    kind_of = [kinds[dy][dx] for dy, dx in OFFSETS]
    kind = kinds[0][0]
    late = sp >= SPACE // 2
    last = sp == LAST_PLANE
    partner = 2 * (SPACE // 2 - 1 - sp // 2) + sp % 2

    def next_head(k):
        return k + 1 - jnp.where(k == SIDE - 1, SIDE, 0)

    gifts = (
        (late, partner, lambda k: k, GUEST),
        (last, SECOND_HOST, next_head, GUEST + 1),
    )
    first_host = jnp.logical_not(late)
    second_host = sp == SECOND_HOST

    @pl.when(first_host)
    def _():
        for t in peers:
            pl.semaphore_signal(
                barrier, inc=1, device_id=(t, partner, dp), device_id_type=MESH
            )

    @pl.when(second_host)
    def _():
        for t in peers:
            pl.semaphore_signal(
                barrier, inc=1, device_id=(t, LAST_PLANE, dp), device_id_type=MESH
            )

    held = len(peers) + rank + jnp.where(late, len(peers), 0)
    held += jnp.where(last, len(peers), 0)

    def announce(r, carry):
        pl.semaphore_signal(
            barrier, inc=1, device_id=(me, r, dp), device_id_type=MESH
        )
        return carry

    lax.fori_loop(rank + 1, SPACE, announce, 0)

    pl.semaphore_wait(barrier, held)

    def enter(r, carry):
        pl.semaphore_signal(
            entered, inc=1, device_id=(me, r, dp), device_id_type=MESH
        )
        return carry

    def send_ssq(r, carry):
        pltpu.make_async_remote_copy(
            ssq_out, ssq_in.at[sp], ssq_send, ssq_recv,
            device_id=(me, r, dp), device_id_type=MESH,
        ).start()
        return carry

    def rows_of(t):
        return pl.ds(pl.multiple_of(t * BLOCK, BLOCK), BLOCK)

    def push(source, target, slot, start, size, to, send, recv):
        pltpu.make_async_remote_copy(
            source(start, size), target(slot, start, size), send, recv.at[slot],
            device_id=to, device_id_type=MESH,
        ).start()

    def block_source(ref, h):
        def at(t):
            def rows(start, size):
                first = pl.multiple_of(t * BLOCK + start, PART)
                return ref(h, pl.ds(first, size))

            return rows

        return at

    def qk_target(slot, start, size):
        return qk_in.at[slot, me, :, pl.ds(start, size)]

    def o_target(slot, start, size):
        return o_in.at[slot, me, pl.ds(start, size)]

    def moves(h, k):
        made = [
            jnp.logical_and(gives, head(k) == h) for gives, _, head, _ in gifts
        ]
        return jnp.logical_or(made[0], made[1])

    def push_main(source, target, h, send, recv):
        for t, k in zip(peers, kind_of):

            @pl.when(jnp.logical_not(moves(h, k)))
            def _():
                push(source(t), target, h, 0, BLOCK, (t, sp, dp), send.at[h], recv)

            @pl.when(moves(h, k))
            def _():
                push(source(t), target, h, PART, BLOCK - PART, (t, sp, dp), send.at[h], recv)

    def push_moved(source, target, h, send, recv, own_send):
        for gives, plane, head, slot in gifts:

            @pl.when(gives)
            def _():
                for t, k in zip(peers, kind_of):

                    @pl.when(head(k) == h)
                    def _():
                        push(source(t), target, slot, 0, PART, (t, plane, dp), send.at[h], recv)

                @pl.when(head(kind) == h)
                def _():
                    push(
                        source(me), target, slot, 0, PART, (me, plane, dp),
                        own_send.at[slot - GUEST], recv,
                    )

    def qk_source(h):
        return block_source(lambda h, rows: proj.at[pl.ds(0, 2), h, rows], h)

    def o_source(h):
        return block_source(lambda h, rows: o_out.at[h, rows], h)

    def send_qk(h):
        push_main(qk_source(h), qk_target, h, qk_send, qk_recv)

    def send_moved_qk(h):
        push_moved(qk_source(h), qk_target, h, qk_send, qk_recv, guest_qk_send)

    send_qk(0)
    lax.fori_loop(0, rank, enter, 0)
    for load in loads[2:]:
        load.start()

    for c in range(2):
        loads[c].wait()
        for r in range(ROWS):
            total = jnp.zeros((128, 128), jnp.float32)
            for h in range(OWN_HEADS):
                part = x[c, h, 128 * r : 128 * (r + 1), :].astype(jnp.float32)
                total += part * part
            ssq_out[r, c : c + 1, :] = jnp.sum(jnp.transpose(total), axis=0, keepdims=True)
    ssq_in[sp] = ssq_out[...]
    lax.fori_loop(0, rank, send_ssq, 0)

    @pl.when(rank < SPACE // 2)
    def _():
        for h in range(1, EARLY_HEADS):
            send_qk(h)

    @pl.when(rank < SPACE - 1)
    def _():
        pl.semaphore_wait(entered, SPACE - 1 - rank)
        lax.fori_loop(rank + 1, SPACE, send_ssq, 0)

    @pl.when(rank >= SPACE // 2)
    def _():
        send_moved_qk(0)
        for h in range(1, EARLY_HEADS):
            send_qk(h)
            send_moved_qk(h)

    for h in range(EARLY_HEADS, OWN_HEADS - 1):
        send_qk(h)
        send_moved_qk(h)
    own = pltpu.make_async_copy(proj.at[pl.ds(0, 2), :, rows_of(me)], own_qk, own_sem)
    own.start()

    for load in loads[3:]:
        load.wait()
    lane = lax.broadcasted_iota(jnp.int32, (1, 128), 1)
    for b in range(GROUPS):
        row = jnp.zeros((1, 128), jnp.int32)
        for i in range(GROUP):
            row = jnp.where(lane % GROUP == i, counts[me * BLOCK + b * GROUP + i], row)
        live[b : b + 1, :] = row
    for f in range(FRAMES):
        scale[pl.ds(0, OWN_HEADS), f : f + 1, :] = steps[:, pl.ds(steps_at[f], 1), :]

    for gives, plane, head, slot in gifts:
        guest = slot - GUEST

        @pl.when(gives)
        def _():
            row = pl.ds(head(kind), 1)
            for c in range(2):
                head_out[guest, c : c + 1, :] = gains[c, row, :]
            for c in range(2, 4):
                head_out[guest, c : c + 1, :] = weight[row, :]
            head_out[guest, 4:8, :] = steps[head(kind)]
            pltpu.make_async_remote_copy(
                head_out.at[guest], head_in.at[guest], head_send.at[guest], head_recv.at[guest],
                device_id=(me, plane, dp), device_id_type=MESH,
            ).start()

    z[...] = jnp.zeros_like(z)

    wait_bytes(ssq_in.at[pl.ds(0, SPACE - 1)], ssq_recv)
    sums = ssq_in[0]
    for s in range(1, SPACE):
        sums += ssq_in[s]
    fac_out[...] = lax.rsqrt(sums / CHANNELS + EPSILON)
    for t in peers:
        pltpu.make_async_remote_copy(
            fac_out.at[t // 2], fac_in.at[me], fac_send, fac_recv,
            device_id=(t, sp, dp), device_id_type=MESH,
        ).start()
    send_qk(OWN_HEADS - 1)
    fac_in[me] = fac_out[me // 2]

    for c in range(2):
        for r in range(ROWS):
            factor = column(fac_out[r, c : c + 1, :])
            for h in range(OWN_HEADS):
                rows = slice(128 * r, 128 * (r + 1))
                part = x[c, h, rows, :].astype(jnp.float32) * factor
                normed[c, h, rows, :] = (part * gains[c, h : h + 1, :]).astype(jnp.bfloat16)

    loads[2].wait()

    def spatial_head(h, carry):
        def tile(i, carry):
            rows = pl.ds(pl.multiple_of(i * QUERY_TILE, QUERY_TILE), QUERY_TILE)
            scores = lax.dot_general(
                normed[0, h, rows, :], normed[1, h], (((1,), (1,)), ((), ())),
                preferred_element_type=jnp.float32,
            )
            top = jnp.max(scores, axis=1, keepdims=True)
            exponent = jnp.exp2((scores - top) * SCALE_LOG2E)
            share = 1.0 / jnp.sum(exponent, axis=1, keepdims=True)
            weights = (exponent * share).astype(jnp.bfloat16)
            o_out[h, rows, :] = jnp.dot(
                weights, x[2, h], preferred_element_type=jnp.float32
            ).astype(jnp.bfloat16)
            return carry

        lax.fori_loop(0, PIXELS // QUERY_TILE, tile, 0)
        push_main(o_source(h), o_target, h, o_send, o_recv)
        push_moved(o_source(h), o_target, h, o_send, o_recv, guest_o_send)
        o_in[h, me] = o_out[h, rows_of(me), :]
        return carry

    lax.fori_loop(0, OWN_HEADS, spatial_head, 0)

    wait_bytes(fac_in.at[pl.ds(0, FRAMES - 1)], fac_recv)
    for c in range(2):
        for f in range(FRAMES):
            fcol[c, f] = column(fac_in[f, c : c + 1, :])
    own.wait()
    for c in range(2):
        for h in range(OWN_HEADS):
            qk_in[h, me, c] = own_qk[c, h]

    for gives, _, head, _ in gifts:

        @pl.when(gives)
        def _():
            none = jnp.zeros((FRAMES, PART, HEAD), jnp.bfloat16)
            for c in range(2):
                qk_in[head(kind), :, c, 0:PART, :] = none
            o_in[head(kind), :, 0:PART, :] = none

    guests = ((first_host, GUEST), (second_host, GUEST + 1))
    for hosts, slot in guests:

        @pl.when(hosts)
        def _():
            wait_bytes(head_in.at[slot - GUEST], head_recv.at[slot - GUEST])

    for hosts, slot in guests:

        @pl.when(hosts)
        def _():
            for f in range(FRAMES):
                row = head_in[slot - GUEST, pl.ds(4 + steps_at[f], 1), :]
                scale[slot, f : f + 1, :] = row

    side = FRAMES * GROUP
    at_row = lax.broadcasted_iota(jnp.int32, (side, side), 0)
    at_lane = lax.broadcasted_iota(jnp.int32, (side, side), 1)
    same = (at_row % GROUP) == (at_lane % GROUP)
    key_frame = at_lane // GROUP
    my_half = pl.ds(pl.multiple_of(half * BLOCK, BLOCK), BLOCK)

    def arrive(part, sems, h):
        less = moves(h, kind)

        @pl.when(jnp.logical_not(less))
        def _():
            wait_bytes(part(h, FRAMES - 1, BLOCK), sems.at[h])

        @pl.when(less)
        def _():
            wait_bytes(part(h, FRAMES - 1, BLOCK - PART), sems.at[h])

    def qk_part(h, frames, rows):
        return qk_in.at[h, pl.ds(0, frames), :, pl.ds(0, rows)]

    def o_part(h, frames, rows):
        return o_in.at[h, pl.ds(0, frames), pl.ds(0, rows)]

    def temporal_weights(h, count, gain):
        wide = []
        for c in range(2):
            factor = fcol[c, :, pl.ds(pl.multiple_of(half * BLOCK, BLOCK), count), :]
            part = qk_in[h, :, c, 0:count, :].astype(jnp.float32) * factor
            wide.append(part * gain(c).reshape(1, 1, HEAD))
        for b in range(count // GROUP):
            queries, keys = (
                w[:, GROUP * b : GROUP * (b + 1), :].reshape(side, HEAD).astype(jnp.bfloat16)
                for w in wide
            )
            scores = lax.dot_general(
                queries, keys, (((1,), (1,)), ((), ())), preferred_element_type=jnp.float32
            )
            seen = same & (key_frame < live[b : b + 1, :])
            scores = jnp.where(seen, scores, -1e30)
            top = jnp.max(scores, axis=1, keepdims=True)
            exponent = jnp.exp2((scores - top) * SCALE_LOG2E)
            share = 1.0 / jnp.sum(exponent, axis=1, keepdims=True)
            mix[h, b] = (exponent * share).astype(jnp.bfloat16)

    def own_weights(h, carry):
        arrive(qk_part, qk_recv, h)
        temporal_weights(h, BLOCK, lambda c: gains[c, pl.ds(h, 1), :])
        return carry

    lax.fori_loop(0, OWN_HEADS, own_weights, 0)
    for hosts, slot in guests:

        @pl.when(hosts)
        def _():
            wait_bytes(qk_part(slot, FRAMES, PART), qk_recv.at[slot])
            temporal_weights(slot, PART, lambda c: head_in[slot - GUEST, c : c + 1, :])

    at_frame = lax.broadcasted_iota(jnp.int32, (FRAMES, GROUP, 128), 0)
    at_lane3 = lax.broadcasted_iota(jnp.int32, (FRAMES, GROUP, 128), 2)
    dot_lane = at_frame == at_lane3
    square_lane = at_frame + FRAMES == at_lane3

    def temporal_head(h, count, own_weight):
        spatial = o_in[h, :, 0:count, :].astype(jnp.float32)
        row_scale = scale[h].reshape(FRAMES, 1, HEAD)
        row_weight = own_weight.reshape(1, 1, HEAD)
        for b in range(count // GROUP):
            pixels = slice(GROUP * b, GROUP * (b + 1))
            block = spatial[:, pixels, :]
            mixed = jnp.dot(
                mix[h, b], block.reshape(side, HEAD).astype(jnp.bfloat16),
                preferred_element_type=jnp.float32,
            ).astype(jnp.bfloat16).astype(jnp.float32)
            modulated = (block + mixed.reshape(FRAMES, GROUP, HEAD)) * row_scale
            dots = jnp.sum(modulated * row_weight, axis=2, keepdims=True)
            squares = jnp.sum(modulated * modulated, axis=2, keepdims=True)
            placed = jnp.where(dot_lane, dots, 0.0) + jnp.where(square_lane, squares, 0.0)
            at = pl.ds(pl.multiple_of(half * BLOCK + GROUP * b, GROUP), GROUP)
            z[at, :] += jnp.sum(placed, axis=0)

    def own_head(h, carry):
        arrive(o_part, o_recv, h)
        temporal_head(h, BLOCK, weight[pl.ds(h, 1), :])
        return carry

    lax.fori_loop(0, OWN_HEADS, own_head, 0)
    for hosts, slot in guests:

        @pl.when(hosts)
        def _():
            wait_bytes(o_part(slot, FRAMES, PART), o_recv.at[slot])
            temporal_head(slot, PART, head_in[slot - GUEST, 2:3, :])

    turned = jnp.transpose(z[...])
    for f in range(FRAMES):
        fin_out[f, 0:1, :] = turned[f : f + 1, :]
        fin_out[f, 1:2, :] = turned[FRAMES + f : FRAMES + f + 1, :]
    owner = me // 2
    slot = half * SPACE + sp
    for t in peers:
        pltpu.make_async_remote_copy(
            fin_out.at[t], fin_in.at[slot], fin_send, fin_recv,
            device_id=(t, owner, dp), device_id_type=MESH,
        ).start()

    @pl.when(sp == owner)
    def _():
        here = pltpu.make_async_copy(fin_out.at[me], fin_in.at[slot], fin_recv)
        here.start()

    @pl.when(sp != owner)
    def _():
        away = pltpu.make_async_remote_copy(
            fin_out.at[me], fin_in.at[slot], last_send, fin_recv,
            device_id=(me, owner, dp), device_id_type=MESH,
        )
        away.start()
        away.wait_send()

    wait_bytes(ssq_in.at[pl.ds(0, SPACE - 1)], ssq_send)
    wait_bytes(fac_in.at[pl.ds(0, FRAMES - 1)], fac_send)
    for h in range(OWN_HEADS):
        wait_bytes(qk_in.at[h, pl.ds(0, FRAMES - 1)], qk_send.at[h])
        wait_bytes(o_in.at[h, pl.ds(0, FRAMES - 1)], o_send.at[h])

    for gives, _, _, slot in gifts:
        guest = slot - GUEST

        @pl.when(gives)
        def _():
            wait_bytes(qk_part(slot, 1, PART), guest_qk_send.at[guest])
            wait_bytes(head_out.at[guest], head_send.at[guest])
            wait_bytes(o_part(slot, 1, PART), guest_o_send.at[guest])

    wait_bytes(fin_out.at[pl.ds(0, FRAMES - 1)], fin_send)
    wait_bytes(fin_in, fin_recv)
    totals = jnp.sum(fin_in[...], axis=0)
    out[...] = totals[0:1, :] * lax.rsqrt(totals[1:2, :] / CHANNELS + EPSILON)


def on_device(projected, q_gain, k_gain, head_weight, step_scale, timestep, frame_count):
    proj = jnp.transpose(projected[0], (1, 2, 0, 3))
    steps = jnp.transpose(step_scale, (1, 0, 2))
    any_space = pl.BlockSpec(memory_space=pl.ANY)
    bf16, f32 = jnp.bfloat16, jnp.float32
    dma = pltpu.SemaphoreType.DMA
    return pl.pallas_call(
        kernel,
        out_shape=jax.ShapeDtypeStruct((1, 128), f32),
        in_specs=[any_space] * 7,
        out_specs=pl.BlockSpec(memory_space=pltpu.VMEM),
        scratch_shapes=[
            pltpu.VMEM((3, OWN_HEADS, PIXELS, HEAD), bf16),
            pltpu.VMEM((SLOTS, FRAMES, 2, BLOCK, HEAD), bf16),
            pltpu.VMEM((2, OWN_HEADS, BLOCK, HEAD), bf16),
            pltpu.VMEM((OWN_HEADS, PIXELS, HEAD), bf16),
            pltpu.VMEM((SLOTS, FRAMES, BLOCK, HEAD), bf16),
            pltpu.VMEM((ROWS, 2, 128), f32),
            pltpu.VMEM((SPACE, ROWS, 2, 128), f32),
            pltpu.VMEM((ROWS, 2, 128), f32),
            pltpu.VMEM((FRAMES, 2, 128), f32),
            pltpu.VMEM((2, OWN_HEADS, PIXELS, HEAD), bf16),
            pltpu.VMEM((2, FRAMES, 128, 128), f32),
            pltpu.VMEM((SLOTS, GROUPS, 128, 128), bf16),
            pltpu.VMEM((SLOTS, FRAMES, HEAD), f32),
            pltpu.VMEM((128, 128), f32),
            pltpu.VMEM((FRAMES, 2, 128), f32),
            pltpu.VMEM((FRAMES, 2, 128), f32),
            pltpu.VMEM((2, OWN_HEADS, HEAD), f32),
            pltpu.VMEM((OWN_HEADS, HEAD), f32),
            pltpu.VMEM((OWN_HEADS, STEPS, HEAD), f32),
            pltpu.VMEM((2, 8, HEAD), f32),
            pltpu.VMEM((2, 8, HEAD), f32),
            pltpu.VMEM((GROUPS, 128), jnp.int32),
            pltpu.SMEM((FRAMES,), jnp.int32),
            pltpu.SMEM((PIXELS,), jnp.int32),
            dma((9,)), dma, dma((OWN_HEADS,)), dma((SLOTS,)), dma, dma, dma, dma,
            dma((OWN_HEADS,)), dma((SLOTS,)), dma, dma, dma,
            pltpu.SemaphoreType.REGULAR, dma((2,)), dma((2,)), dma((2,)), dma((2,)),
        ],
        compiler_params=pltpu.CompilerParams(
            collective_id=0, has_side_effects=True, vmem_limit_bytes=56 * 2**20
        ),
        cost_estimate=pl.CostEstimate(
            flops=3_000_000_000, bytes_accessed=8_000_000, transcendentals=6_000_000
        ),
        name="space_time_attention",
    )(proj, q_gain, k_gain, head_weight, steps, timestep, frame_count)


def solution(mesh):
    in_specs = (
        P(("dp", "tm"), None, None, "space", None),
        P("space", None),
        P("space", None),
        P("space", None),
        P(None, "space", None),
        P("dp"),
        P("dp"),
    )
    out_specs = P(("dp", "tm"), "space")
    return jax.shard_map(
        on_device, mesh=mesh, in_specs=in_specs, out_specs=out_specs, check_vma=False
    )
```

```python
import functools
import math

import jax
import jax.numpy as jnp
from jax import lax
from jax.experimental import pallas as pl
from jax.experimental.pallas import tpu as pltpu
from jax.sharding import PartitionSpec as P

HEADS = 40
HEAD = 128
PIXELS = 1024
FRAMES = 16
STEPS = 4
SPACE = 8
OWN_HEADS = HEADS // SPACE
BLOCK = PIXELS // FRAMES
ROWS = PIXELS // 128
QUERY_TILE = 256
GROUP = 8
GROUPS = BLOCK // GROUP
EARLY_HEADS = 3
SIDE = 4
GUEST = OWN_HEADS
SLOTS = OWN_HEADS + 2
HALF = BLOCK // 2
LAST_PLANE = 4
SECOND_HOST = 1
PART = 16

EPSILON = 1e-06
CHANNELS = HEADS * HEAD
SCALE_LOG2E = HEAD ** (-0.5) * math.log2(math.e)
MESH = pl.DeviceIdType.MESH


OFFSETS = (
    (2, 2), (2, 3), (2, 1), (3, 2), (1, 2), (2, 0), (0, 2), (3, 1),
    (1, 3), (3, 3), (1, 1), (3, 0), (1, 0), (0, 3), (0, 1),
)


def wait_bytes(ref, sem):
    pltpu.make_async_copy(ref, ref, sem).wait()


def column(row):
    return jnp.transpose(jnp.broadcast_to(row, (128, 128)))


def kernel(
    proj, q_gain, k_gain, head_weight, step_scale, timestep, frame_count,
    out,
    x, qk_in, own_qk, o_out, o_in, ssq_out, ssq_in, fac_out, fac_in, normed, fcol, mix, scale, z,
    fin_out, fin_in, gains, weight, steps, head_out, head_in, live, steps_at, counts,
    local_sem, own_sem, qk_send, qk_recv, ssq_send, ssq_recv, fac_send, fac_recv,
    o_send, o_recv, fin_send, fin_recv, last_send, half_recv, entered, guest_qk_send, guest_o_send, head_send, head_recv,
):
    me = lax.axis_index("tm")
    sp = lax.axis_index("space")
    dp = lax.axis_index("dp")
    y, xx = me // SIDE, me % SIDE
    down = [jnp.where(y + d >= SIDE, y + d - SIDE, y + d) for d in range(SIDE)]
    along = [jnp.where(xx + d >= SIDE, xx + d - SIDE, xx + d) for d in range(SIDE)]
    peers = [SIDE * down[dy] + along[dx] for dy, dx in OFFSETS]
    half = me % 2

    loads = [
        pltpu.make_async_copy(proj.at[0], x.at[0], local_sem.at[0]),
        pltpu.make_async_copy(proj.at[1], x.at[1], local_sem.at[1]),
        pltpu.make_async_copy(proj.at[2], x.at[2], local_sem.at[2]),
        pltpu.make_async_copy(q_gain, gains.at[0], local_sem.at[3]),
        pltpu.make_async_copy(k_gain, gains.at[1], local_sem.at[4]),
        pltpu.make_async_copy(head_weight, weight, local_sem.at[5]),
        pltpu.make_async_copy(step_scale, steps, local_sem.at[6]),
        pltpu.make_async_copy(timestep, steps_at, local_sem.at[7]),
        pltpu.make_async_copy(frame_count, counts, local_sem.at[8]),
    ]
    for load in loads[:2]:
        load.start()

    barrier = pltpu.get_barrier_semaphore()
    for t in peers:
        pl.semaphore_signal(barrier, inc=1, device_id=(t, sp, dp), device_id_type=MESH)
    rank = sp

    kinds = [[v + u - jnp.where(v + u >= SIDE, SIDE, 0) for u in along] for v in down]
    kind_of = [kinds[dy][dx] for dy, dx in OFFSETS]
    kind = kinds[0][0]
    late = sp >= SPACE // 2
    last = sp == LAST_PLANE
    partner = 2 * (SPACE // 2 - 1 - sp // 2) + sp % 2

    def next_head(k):
        return k + 1 - jnp.where(k == SIDE - 1, SIDE, 0)

    gifts = (
        (late, partner, lambda k: k, GUEST),
        (last, SECOND_HOST, next_head, GUEST + 1),
    )
    first_host = jnp.logical_not(late)
    second_host = sp == SECOND_HOST

    @pl.when(first_host)
    def _():
        for t in peers:
            pl.semaphore_signal(
                barrier, inc=1, device_id=(t, partner, dp), device_id_type=MESH
            )

    @pl.when(second_host)
    def _():
        for t in peers:
            pl.semaphore_signal(
                barrier, inc=1, device_id=(t, LAST_PLANE, dp), device_id_type=MESH
            )

    held = len(peers) + rank + jnp.where(late, len(peers), 0)
    held += jnp.where(last, len(peers), 0)

    def announce(r, carry):
        pl.semaphore_signal(
            barrier, inc=1, device_id=(me, r, dp), device_id_type=MESH
        )
        return carry

    lax.fori_loop(rank + 1, SPACE, announce, 0)

    pl.semaphore_wait(barrier, held)

    def enter(r, carry):
        pl.semaphore_signal(
            entered, inc=1, device_id=(me, r, dp), device_id_type=MESH
        )
        return carry

    def send_ssq(r, carry):
        pltpu.make_async_remote_copy(
            ssq_out, ssq_in.at[sp], ssq_send, ssq_recv,
            device_id=(me, r, dp), device_id_type=MESH,
        ).start()
        return carry

    def rows_of(t):
        return pl.ds(pl.multiple_of(t * BLOCK, BLOCK), BLOCK)

    def push(source, target, slot, start, size, to, send, recv):
        pltpu.make_async_remote_copy(
            source(start, size), target(slot, start, size), send, recv.at[slot],
            device_id=to, device_id_type=MESH,
        ).start()

    def block_source(ref, h):
        def at(t):
            def rows(start, size):
                first = pl.multiple_of(t * BLOCK + start, PART)
                return ref(h, pl.ds(first, size))

            return rows

        return at

    def qk_target(slot, start, size):
        return qk_in.at[slot, me, :, pl.ds(start, size)]

    def o_target(slot, start, size):
        return o_in.at[slot, me, pl.ds(start, size)]

    def moves(h, k):
        made = [
            jnp.logical_and(gives, head(k) == h) for gives, _, head, _ in gifts
        ]
        return jnp.logical_or(made[0], made[1])

    def push_main(source, target, h, send, recv):
        for t, k in zip(peers, kind_of):

            @pl.when(jnp.logical_not(moves(h, k)))
            def _():
                push(source(t), target, h, 0, BLOCK, (t, sp, dp), send.at[h], recv)

            @pl.when(moves(h, k))
            def _():
                push(source(t), target, h, PART, BLOCK - PART, (t, sp, dp), send.at[h], recv)

    def push_moved(source, target, h, send, recv, own_send):
        for gives, plane, head, slot in gifts:

            @pl.when(gives)
            def _():
                for t, k in zip(peers, kind_of):

                    @pl.when(head(k) == h)
                    def _():
                        push(source(t), target, slot, 0, PART, (t, plane, dp), send.at[h], recv)

                @pl.when(head(kind) == h)
                def _():
                    push(
                        source(me), target, slot, 0, PART, (me, plane, dp),
                        own_send.at[slot - GUEST], recv,
                    )

    def qk_source(h):
        return block_source(lambda h, rows: proj.at[pl.ds(0, 2), h, rows], h)

    def o_source(h):
        return block_source(lambda h, rows: o_out.at[h, rows], h)

    def send_qk(h):
        push_main(qk_source(h), qk_target, h, qk_send, qk_recv)

    def send_moved_qk(h):
        push_moved(qk_source(h), qk_target, h, qk_send, qk_recv, guest_qk_send)

    send_qk(0)
    lax.fori_loop(0, rank, enter, 0)
    for load in loads[2:]:
        load.start()

    for c in range(2):
        loads[c].wait()
        for r in range(ROWS):
            total = jnp.zeros((128, 128), jnp.float32)
            for h in range(OWN_HEADS):
                part = x[c, h, 128 * r : 128 * (r + 1), :].astype(jnp.float32)
                total += part * part
            ssq_out[r, c : c + 1, :] = jnp.sum(jnp.transpose(total), axis=0, keepdims=True)
    ssq_in[sp] = ssq_out[...]
    lax.fori_loop(0, rank, send_ssq, 0)

    @pl.when(rank < SPACE // 2)
    def _():
        for h in range(1, EARLY_HEADS):
            send_qk(h)

    @pl.when(rank < SPACE - 1)
    def _():
        pl.semaphore_wait(entered, SPACE - 1 - rank)
        lax.fori_loop(rank + 1, SPACE, send_ssq, 0)

    @pl.when(rank >= SPACE // 2)
    def _():
        send_moved_qk(0)
        for h in range(1, EARLY_HEADS):
            send_qk(h)
            send_moved_qk(h)

    for h in range(EARLY_HEADS, OWN_HEADS - 1):
        send_qk(h)
        send_moved_qk(h)
    own = pltpu.make_async_copy(proj.at[pl.ds(0, 2), :, rows_of(me)], own_qk, own_sem)
    own.start()

    for load in loads[3:]:
        load.wait()
    lane = lax.broadcasted_iota(jnp.int32, (1, 128), 1)
    for b in range(GROUPS):
        row = jnp.zeros((1, 128), jnp.int32)
        for i in range(GROUP):
            row = jnp.where(lane % GROUP == i, counts[me * BLOCK + b * GROUP + i], row)
        live[b : b + 1, :] = row
    for f in range(FRAMES):
        scale[pl.ds(0, OWN_HEADS), f : f + 1, :] = steps[:, pl.ds(steps_at[f], 1), :]

    for gives, plane, head, slot in gifts:
        guest = slot - GUEST

        @pl.when(gives)
        def _():
            row = pl.ds(head(kind), 1)
            for c in range(2):
                head_out[guest, c : c + 1, :] = gains[c, row, :]
            for c in range(2, 4):
                head_out[guest, c : c + 1, :] = weight[row, :]
            head_out[guest, 4:8, :] = steps[head(kind)]
            pltpu.make_async_remote_copy(
                head_out.at[guest], head_in.at[guest], head_send.at[guest], head_recv.at[guest],
                device_id=(me, plane, dp), device_id_type=MESH,
            ).start()

    z[...] = jnp.zeros_like(z)

    wait_bytes(ssq_in.at[pl.ds(0, SPACE - 1)], ssq_recv)
    sums = ssq_in[0]
    for s in range(1, SPACE):
        sums += ssq_in[s]
    fac_out[...] = lax.rsqrt(sums / CHANNELS + EPSILON)
    for t in peers:
        pltpu.make_async_remote_copy(
            fac_out.at[t // 2], fac_in.at[me], fac_send, fac_recv,
            device_id=(t, sp, dp), device_id_type=MESH,
        ).start()
    send_qk(OWN_HEADS - 1)
    fac_in[me] = fac_out[me // 2]

    for c in range(2):
        for r in range(ROWS):
            factor = column(fac_out[r, c : c + 1, :])
            for h in range(OWN_HEADS):
                rows = slice(128 * r, 128 * (r + 1))
                part = x[c, h, rows, :].astype(jnp.float32) * factor
                normed[c, h, rows, :] = (part * gains[c, h : h + 1, :]).astype(jnp.bfloat16)

    loads[2].wait()

    def spatial_head(h, carry):
        def tile(i, carry):
            rows = pl.ds(pl.multiple_of(i * QUERY_TILE, QUERY_TILE), QUERY_TILE)
            scores = lax.dot_general(
                normed[0, h, rows, :], normed[1, h], (((1,), (1,)), ((), ())),
                preferred_element_type=jnp.float32,
            )
            top = jnp.max(scores, axis=1, keepdims=True)
            exponent = jnp.exp2((scores - top) * SCALE_LOG2E)
            share = 1.0 / jnp.sum(exponent, axis=1, keepdims=True)
            weights = (exponent * share).astype(jnp.bfloat16)
            o_out[h, rows, :] = jnp.dot(
                weights, x[2, h], preferred_element_type=jnp.float32
            ).astype(jnp.bfloat16)
            return carry

        lax.fori_loop(0, PIXELS // QUERY_TILE, tile, 0)
        @pl.when(h < OWN_HEADS - 1)
        def _():
            push_main(o_source(h), o_target, h, o_send, o_recv)
            push_moved(o_source(h), o_target, h, o_send, o_recv, guest_o_send)

        @pl.when(h == OWN_HEADS - 1)
        def _():
            for start, sem in ((0, o_recv.at[OWN_HEADS - 1]), (HALF, half_recv)):
                for t in peers:
                    pltpu.make_async_remote_copy(
                        o_source(OWN_HEADS - 1)(t)(start, HALF),
                        o_target(OWN_HEADS - 1, start, HALF), o_send.at[OWN_HEADS - 1], sem,
                        device_id=(t, sp, dp), device_id_type=MESH,
                    ).start()

        o_in[h, me] = o_out[h, rows_of(me), :]
        return carry

    lax.fori_loop(0, OWN_HEADS, spatial_head, 0)

    wait_bytes(fac_in.at[pl.ds(0, FRAMES - 1)], fac_recv)
    for c in range(2):
        for f in range(FRAMES):
            fcol[c, f] = column(fac_in[f, c : c + 1, :])
    own.wait()
    for c in range(2):
        for h in range(OWN_HEADS):
            qk_in[h, me, c] = own_qk[c, h]

    for gives, _, head, _ in gifts:

        @pl.when(gives)
        def _():
            none = jnp.zeros((FRAMES, PART, HEAD), jnp.bfloat16)
            for c in range(2):
                qk_in[head(kind), :, c, 0:PART, :] = none
            o_in[head(kind), :, 0:PART, :] = none

    guests = ((first_host, GUEST), (second_host, GUEST + 1))
    for hosts, slot in guests:

        @pl.when(hosts)
        def _():
            wait_bytes(head_in.at[slot - GUEST], head_recv.at[slot - GUEST])

    for hosts, slot in guests:

        @pl.when(hosts)
        def _():
            for f in range(FRAMES):
                row = head_in[slot - GUEST, pl.ds(4 + steps_at[f], 1), :]
                scale[slot, f : f + 1, :] = row

    side = FRAMES * GROUP
    at_row = lax.broadcasted_iota(jnp.int32, (side, side), 0)
    at_lane = lax.broadcasted_iota(jnp.int32, (side, side), 1)
    same = (at_row % GROUP) == (at_lane % GROUP)
    key_frame = at_lane // GROUP
    my_half = pl.ds(pl.multiple_of(half * BLOCK, BLOCK), BLOCK)

    def arrive(part, sems, h):
        less = moves(h, kind)

        @pl.when(jnp.logical_not(less))
        def _():
            wait_bytes(part(h, FRAMES - 1, BLOCK), sems.at[h])

        @pl.when(less)
        def _():
            wait_bytes(part(h, FRAMES - 1, BLOCK - PART), sems.at[h])

    def qk_part(h, frames, rows):
        return qk_in.at[h, pl.ds(0, frames), :, pl.ds(0, rows)]

    def o_part(h, frames, rows):
        return o_in.at[h, pl.ds(0, frames), pl.ds(0, rows)]

    def temporal_weights(h, count, gain):
        wide = []
        for c in range(2):
            factor = fcol[c, :, pl.ds(pl.multiple_of(half * BLOCK, BLOCK), count), :]
            part = qk_in[h, :, c, 0:count, :].astype(jnp.float32) * factor
            wide.append(part * gain(c).reshape(1, 1, HEAD))
        for b in range(count // GROUP):
            queries, keys = (
                w[:, GROUP * b : GROUP * (b + 1), :].reshape(side, HEAD).astype(jnp.bfloat16)
                for w in wide
            )
            scores = lax.dot_general(
                queries, keys, (((1,), (1,)), ((), ())), preferred_element_type=jnp.float32
            )
            seen = same & (key_frame < live[b : b + 1, :])
            scores = jnp.where(seen, scores, -1e30)
            top = jnp.max(scores, axis=1, keepdims=True)
            exponent = jnp.exp2((scores - top) * SCALE_LOG2E)
            share = 1.0 / jnp.sum(exponent, axis=1, keepdims=True)
            mix[h, b] = (exponent * share).astype(jnp.bfloat16)

    def own_weights(h, carry):
        arrive(qk_part, qk_recv, h)
        temporal_weights(h, BLOCK, lambda c: gains[c, pl.ds(h, 1), :])
        return carry

    lax.fori_loop(0, OWN_HEADS, own_weights, 0)
    for hosts, slot in guests:

        @pl.when(hosts)
        def _():
            wait_bytes(qk_part(slot, FRAMES, PART), qk_recv.at[slot])
            temporal_weights(slot, PART, lambda c: head_in[slot - GUEST, c : c + 1, :])

    at_frame = lax.broadcasted_iota(jnp.int32, (FRAMES, GROUP, 128), 0)
    at_lane3 = lax.broadcasted_iota(jnp.int32, (FRAMES, GROUP, 128), 2)
    dot_lane = at_frame == at_lane3
    square_lane = at_frame + FRAMES == at_lane3

    def temporal_head(h, count, own_weight, start=0):
        spatial = o_in[h, :, start : start + count, :].astype(jnp.float32)
        row_scale = scale[h].reshape(FRAMES, 1, HEAD)
        row_weight = own_weight.reshape(1, 1, HEAD)
        for b in range(count // GROUP):
            pixels = slice(GROUP * b, GROUP * (b + 1))
            block = spatial[:, pixels, :]
            mixed = jnp.dot(
                mix[h, start // GROUP + b], block.reshape(side, HEAD).astype(jnp.bfloat16),
                preferred_element_type=jnp.float32,
            ).astype(jnp.bfloat16).astype(jnp.float32)
            modulated = (block + mixed.reshape(FRAMES, GROUP, HEAD)) * row_scale
            dots = jnp.sum(modulated * row_weight, axis=2, keepdims=True)
            squares = jnp.sum(modulated * modulated, axis=2, keepdims=True)
            placed = jnp.where(dot_lane, dots, 0.0) + jnp.where(square_lane, squares, 0.0)
            at = pl.ds(pl.multiple_of(half * BLOCK + start + GROUP * b, GROUP), GROUP)
            z[at, :] += jnp.sum(placed, axis=0)

    def own_head(h, carry):
        arrive(o_part, o_recv, h)
        temporal_head(h, BLOCK, weight[pl.ds(h, 1), :])
        return carry

    lax.fori_loop(0, OWN_HEADS - 1, own_head, 0)
    end = OWN_HEADS - 1
    for start, sem in ((0, o_recv.at[end]), (HALF, half_recv)):
        wait_bytes(o_in.at[end, pl.ds(0, FRAMES - 1), pl.ds(start, HALF)], sem)
        temporal_head(end, HALF, weight[end : end + 1, :], start)

    for hosts, slot in guests:

        @pl.when(hosts)
        def _():
            wait_bytes(o_part(slot, FRAMES, PART), o_recv.at[slot])
            temporal_head(slot, PART, head_in[slot - GUEST, 2:3, :])

    turned = jnp.transpose(z[...])
    for f in range(FRAMES):
        fin_out[f, 0:1, :] = turned[f : f + 1, :]
        fin_out[f, 1:2, :] = turned[FRAMES + f : FRAMES + f + 1, :]
    owner = me // 2
    slot = half * SPACE + sp
    for t in peers:
        pltpu.make_async_remote_copy(
            fin_out.at[t], fin_in.at[slot], fin_send, fin_recv,
            device_id=(t, owner, dp), device_id_type=MESH,
        ).start()

    @pl.when(sp == owner)
    def _():
        here = pltpu.make_async_copy(fin_out.at[me], fin_in.at[slot], fin_recv)
        here.start()

    @pl.when(sp != owner)
    def _():
        away = pltpu.make_async_remote_copy(
            fin_out.at[me], fin_in.at[slot], last_send, fin_recv,
            device_id=(me, owner, dp), device_id_type=MESH,
        )
        away.start()
        away.wait_send()

    wait_bytes(ssq_in.at[pl.ds(0, SPACE - 1)], ssq_send)
    wait_bytes(fac_in.at[pl.ds(0, FRAMES - 1)], fac_send)
    for h in range(OWN_HEADS):
        wait_bytes(qk_in.at[h, pl.ds(0, FRAMES - 1)], qk_send.at[h])
        wait_bytes(o_in.at[h, pl.ds(0, FRAMES - 1)], o_send.at[h])

    for gives, _, _, slot in gifts:
        guest = slot - GUEST

        @pl.when(gives)
        def _():
            wait_bytes(qk_part(slot, 1, PART), guest_qk_send.at[guest])
            wait_bytes(head_out.at[guest], head_send.at[guest])
            wait_bytes(o_part(slot, 1, PART), guest_o_send.at[guest])

    wait_bytes(fin_out.at[pl.ds(0, FRAMES - 1)], fin_send)
    wait_bytes(fin_in, fin_recv)
    totals = jnp.sum(fin_in[...], axis=0)
    out[...] = totals[0:1, :] * lax.rsqrt(totals[1:2, :] / CHANNELS + EPSILON)


def on_device(projected, q_gain, k_gain, head_weight, step_scale, timestep, frame_count):
    proj = jnp.transpose(projected[0], (1, 2, 0, 3))
    steps = jnp.transpose(step_scale, (1, 0, 2))
    any_space = pl.BlockSpec(memory_space=pl.ANY)
    bf16, f32 = jnp.bfloat16, jnp.float32
    dma = pltpu.SemaphoreType.DMA
    return pl.pallas_call(
        kernel,
        out_shape=jax.ShapeDtypeStruct((1, 128), f32),
        in_specs=[any_space] * 7,
        out_specs=pl.BlockSpec(memory_space=pltpu.VMEM),
        scratch_shapes=[
            pltpu.VMEM((3, OWN_HEADS, PIXELS, HEAD), bf16),
            pltpu.VMEM((SLOTS, FRAMES, 2, BLOCK, HEAD), bf16),
            pltpu.VMEM((2, OWN_HEADS, BLOCK, HEAD), bf16),
            pltpu.VMEM((OWN_HEADS, PIXELS, HEAD), bf16),
            pltpu.VMEM((SLOTS, FRAMES, BLOCK, HEAD), bf16),
            pltpu.VMEM((ROWS, 2, 128), f32),
            pltpu.VMEM((SPACE, ROWS, 2, 128), f32),
            pltpu.VMEM((ROWS, 2, 128), f32),
            pltpu.VMEM((FRAMES, 2, 128), f32),
            pltpu.VMEM((2, OWN_HEADS, PIXELS, HEAD), bf16),
            pltpu.VMEM((2, FRAMES, 128, 128), f32),
            pltpu.VMEM((SLOTS, GROUPS, 128, 128), bf16),
            pltpu.VMEM((SLOTS, FRAMES, HEAD), f32),
            pltpu.VMEM((128, 128), f32),
            pltpu.VMEM((FRAMES, 2, 128), f32),
            pltpu.VMEM((FRAMES, 2, 128), f32),
            pltpu.VMEM((2, OWN_HEADS, HEAD), f32),
            pltpu.VMEM((OWN_HEADS, HEAD), f32),
            pltpu.VMEM((OWN_HEADS, STEPS, HEAD), f32),
            pltpu.VMEM((2, 8, HEAD), f32),
            pltpu.VMEM((2, 8, HEAD), f32),
            pltpu.VMEM((GROUPS, 128), jnp.int32),
            pltpu.SMEM((FRAMES,), jnp.int32),
            pltpu.SMEM((PIXELS,), jnp.int32),
            dma((9,)), dma, dma((OWN_HEADS,)), dma((SLOTS,)), dma, dma, dma, dma,
            dma((OWN_HEADS,)), dma((SLOTS,)), dma, dma, dma,
            dma,
            pltpu.SemaphoreType.REGULAR, dma((2,)), dma((2,)), dma((2,)), dma((2,)),
        ],
        compiler_params=pltpu.CompilerParams(
            collective_id=0, has_side_effects=True, vmem_limit_bytes=56 * 2**20
        ),
        cost_estimate=pl.CostEstimate(
            flops=3_000_000_000, bytes_accessed=8_000_000, transcendentals=6_000_000
        ),
        name="space_time_attention",
    )(proj, q_gain, k_gain, head_weight, steps, timestep, frame_count)


def solution(mesh):
    in_specs = (
        P(("dp", "tm"), None, None, "space", None),
        P("space", None),
        P("space", None),
        P("space", None),
        P(None, "space", None),
        P("dp"),
        P("dp"),
    )
    out_specs = P(("dp", "tm"), "space")
    return jax.shard_map(
        on_device, mesh=mesh, in_specs=in_specs, out_specs=out_specs, check_vma=False
    )
```
